512 devices in a mesh: seq: 64 (over y_lo, z, x), head: 8 (over y_hi, core).
Axes of the slice: x: 4, y: 8 (y_hi: 4, y_lo: 2; y = y_hi * 2 + y_lo), z: 8, core: 2. Of those that a mesh axis runs over, the one named last changes fastest.
Arguments:
- qkv: bfloat16 [3, 32768, 3072], P(None, ('seq', 'head')), may hold values from -6 to 6
- text_kv: bfloat16 [2, 256, 3072], P(None, None, 'head'), may hold values from -6 to 6
- window_mask: int32 [128, 27], P('seq'), may hold values from 0 to 1, as said below
Outputs:
- attended: bfloat16 [32768, 3072], P(('seq', 'head'))
The draws below stay inside these ranges and needn't reach their ends.
Inputs may be any that keep to these rules, and one draw needn't show every extreme that they name: `window_mask`: each entry is 1 for offset 13 (the query's own tile) and 0 wherever the offset leads outside the grid.
All inputs are finite; a program needn't handle non-finite values.
Results may differ from the reference program's by a relative error of at most 0.0049.
Values may be sent and summed in bfloat16 or wider, within the bound.
A program may use at most 128 MiB of HBM per device.

```python
import math
import jax
import jax.numpy as jnp
from jax import lax

D = 3072
HEADS = 24
HEAD_DIM = 128
TILE = 256
GW = 8
TT = 2
TXT = 256
GH = 8
TOKENS = 32768


def draw_qkv(key, part):
    key = jax.random.fold_in(key, 11)
    first = jax.random.fold_in(key, 0)
    total = GH * GW * TT * TILE
    values = jnp.clip(jax.random.normal(first, (3, total, D), jnp.float32), -6.0, 6.0)
    return values.astype(jnp.bfloat16)


def draw_window_mask(key, part):
    key = jax.random.fold_in(key, 5)
    count = GH * GW * TT
    tile_ids = jnp.arange(count, dtype=jnp.int32)[:, None]
    column_id = tile_ids // TT
    frame = tile_ids % TT
    tile_row = column_id // GW
    tile_col = column_id % GW
    offset = jnp.arange(27, dtype=jnp.int32)[None, :]
    frame_step = offset // 9 - 1
    row_step = offset // 3 % 3 - 1
    col_step = offset % 3 - 1
    inside = (frame + frame_step >= 0) & (frame + frame_step < TT)
    inside = inside & (tile_row + row_step >= 0) & (tile_row + row_step < GH)
    inside = inside & (tile_col + col_step >= 0) & (tile_col + col_step < GW)
    keep = jax.random.randint(key, (count, 27), 0, 10) < 7
    return jnp.where(inside & (keep | (offset == 13)), 1, 0).astype(jnp.int32)


def block_levels(stream_key, shape, shards, least, high):
    def one(dim, blocks):
        draws = jax.random.uniform(jax.random.fold_in(jax.random.fold_in(stream_key, 6), dim), (blocks,), jnp.float32, least / len(shards), high / len(shards))
        return jnp.repeat(jnp.exp(draws), shape[dim] // blocks).reshape((-1,) + (1,) * (len(shape) - dim - 1))

    gain = one(*shards[0])
    for cut in shards[1:]:
        gain = gain * one(*cut)
    return gain


def gaussian(key, dims, deviation, most, cuts=(), held_as=jnp.bfloat16):
    array = deviation * jax.random.normal(key, dims, jnp.float32)
    if cuts:
        array = array * block_levels(key, dims, cuts, -0.22, 0.18)
    return jnp.clip(array, -most, most).astype(held_as)


def setup_inputs(seed: int = 0) -> dict:
    streams_of = jax.random.split(jax.random.key(seed), 4)
    qkv = draw_qkv(jax.random.fold_in(streams_of[3], 71), 0)
    text_kv = gaussian(streams_of[1], (2, TXT, D), 1.0, 6.0, ((2, 8),))
    window_mask = draw_window_mask(jax.random.fold_in(streams_of[3], 71), 0)
    return dict(qkv=qkv, text_kv=text_kv, window_mask=window_mask)


def visible_tiles(mask_rows, count):
    query_tile = jnp.arange(count, dtype=jnp.int32)[:, None, None]
    piece = jnp.arange(9, dtype=jnp.int32)[None, :, None]
    key_tile = jnp.arange(count, dtype=jnp.int32)[None, None, :]
    delta = key_tile - query_tile
    offset = (delta + 1) * 9 + piece
    table = (offset[..., None] == jnp.arange(27, dtype=jnp.int32)).astype(jnp.int32)
    picked = lax.optimization_barrier(jnp.sum(table * mask_rows[:, None, None, :], axis=-1))
    usable = (picked > 0) & (jnp.abs(delta) <= 1)
    return jnp.transpose(usable, (1, 0, 2))

def reference(qkv, text_kv, window_mask):
    rows = TT * TILE
    query, keys, values = (qkv[0], qkv[1], qkv[2])

    def padded_grid(field):
        shaped = field.reshape(GH, GW, rows, D)
        return jnp.pad(shaped, ((1, 1), (1, 1), (0, 0), (0, 0)))
    key_grid = padded_grid(keys)
    value_grid = padded_grid(values)
    scale = 1.0 / math.sqrt(HEAD_DIM)
    text_keys = text_kv[0].astype(jnp.float32).reshape(TXT, HEADS, HEAD_DIM)
    text_vals = text_kv[1].astype(jnp.float32).reshape(TXT, HEADS, HEAD_DIM)

    def column(index):
        row_pos = index // GW
        col_pos = index % GW
        start = (index * rows).astype(jnp.int32)
        local_q = lax.dynamic_slice_in_dim(query, start, rows, 0).astype(jnp.float32).reshape(rows, HEADS, HEAD_DIM)
        zero = jnp.int32(0)
        near_k = lax.dynamic_slice(key_grid, (row_pos, col_pos, zero, zero), (3, 3, rows, D))
        near_v = lax.dynamic_slice(value_grid, (row_pos, col_pos, zero, zero), (3, 3, rows, D))
        near_k = near_k.reshape(9 * rows, HEADS, HEAD_DIM).astype(jnp.float32)
        near_v = near_v.reshape(9 * rows, HEADS, HEAD_DIM).astype(jnp.float32)
        mask_rows = lax.dynamic_slice_in_dim(window_mask, (index * TT).astype(jnp.int32), TT, 0)
        tiles = visible_tiles(mask_rows, TT)
        allowed = jnp.repeat(jnp.repeat(tiles, TILE, axis=1), TILE, axis=2)
        allowed = jnp.transpose(allowed, (1, 0, 2)).reshape(rows, 9 * rows)
        allowed = jnp.concatenate([jnp.ones((rows, TXT), dtype=bool), allowed], axis=1)
        all_keys = jnp.concatenate([text_keys, near_k], axis=0)
        all_vals = jnp.concatenate([text_vals, near_v], axis=0)
        score = jnp.einsum('qhd,khd->hqk', local_q, all_keys) * scale
        score = jnp.where(allowed[None], score, -1e+30)
        largest = lax.optimization_barrier(jnp.max(score, axis=-1, keepdims=True))
        expo = jnp.exp(score - largest)
        total = lax.optimization_barrier(jnp.sum(expo, axis=-1, keepdims=True))
        weight = lax.optimization_barrier((expo / total).astype(jnp.bfloat16)).astype(jnp.float32)
        result = jnp.einsum('hqk,khd->qhd', weight, all_vals)
        return result.reshape(rows, D).astype(jnp.bfloat16)
    outputs = lax.map(column, jnp.arange(GH * GW, dtype=jnp.int32))
    return outputs.reshape(TOKENS, D)
```

```python
import functools
import math

import jax
import jax.numpy as jnp
from jax import lax
from jax.experimental import pallas as pl
from jax.experimental.pallas import tpu as pltpu
from jax.sharding import PartitionSpec as P

HEAD_DIM = 128
GW = 8
CORES = 2
MESH = pl.DeviceIdType.MESH
NEG = -1e30
C2 = math.log2(math.e) / math.sqrt(HEAD_DIM)
F32 = jnp.float32


def kernel(
    grid_rows, nh, hd,
    qkv, text, mask, out,
    q_s, kv_s, text_s, mask_s, bias_s, m_s, l_s, acc_s, osend_s, orecv_s, lsend_s, lrecv_s, ofin_s,
    own_sem, kv_sem, q_sem, text_sem, a2a_send,
    z_send, z_recv, x_send, x_recv, mk_send, mk_recv, o_send, o_recv, ls_send, ls_recv, out_send, out_sem,
):
    s, my = lax.axis_index("seq"), lax.axis_index("head")
    row, col = s // GW, s % GW
    rows = qkv.shape[1]
    total = rows * nh
    tile = total // 2
    width = hd * HEAD_DIM
    quarters = nh // CORES
    part = rows * CORES
    core, hi = my % CORES, my // CORES
    has_q = [None, col > 0, col < GW - 1]
    has_kv = [None, row > 0, row < grid_rows - 1]
    q_dev = [None, (s - 1, my), (s + 1, my)]
    kv_dev = [None, (s - GW, my), (s + GW, my)]
    peers = [(0, (hi * CORES + 1 - core))]
    for r in [d for d in range(1, quarters) if 2 * d != quarters] + [d for d in range(1, quarters) if 2 * d == quarters]:
        for other in range(CORES):
            peers.append((r, ((hi + r) % quarters) * CORES + (core + other) % CORES))
    my_rows = pl.ds(pl.multiple_of(my * rows, rows), rows)

    def lanes(h, i, n=1):
        return pl.ds(pl.multiple_of((h * hd + i) * HEAD_DIM, HEAD_DIM), n * HEAD_DIM)

    def at(i, n=1):
        return pl.ds(i * HEAD_DIM, n * HEAD_DIM)

    def remote(src, dst, ssem, rsem, dev):
        pltpu.make_async_remote_copy(
            src_ref=src, dst_ref=dst, send_sem=ssem, recv_sem=rsem, device_id=dev, device_id_type=MESH
        ).start()

    def wait(ref, sem):
        pltpu.make_async_copy(ref, ref, sem).wait()

    pltpu.make_async_copy(qkv.at[pl.ds(1, 2), :, lanes(my, 0, hd)], kv_s.at[0, :, my_rows, :], own_sem).start()
    for i in range(hd):
        pltpu.make_async_copy(qkv.at[0, :, lanes(my, i)], q_s.at[0, my_rows, at(i)], q_sem.at[i]).start()
    pltpu.make_async_copy(text, text_s, text_sem).start()

    barrier = pltpu.get_barrier_semaphore()
    count = len(peers)
    for _, p in peers:
        pl.semaphore_signal(barrier, inc=1, device_id=(s, p), device_id_type=MESH)
    for has, dev in zip(has_q[1:] + has_kv[1:], q_dev[1:] + kv_dev[1:]):
        count = count + has.astype(jnp.int32)

        @pl.when(has)
        def _():
            pl.semaphore_signal(barrier, inc=1, device_id=dev, device_id_type=MESH)

    mask_s[0] = jnp.zeros_like(mask_s[0])
    mask_s[0, 0:2, 0:27] = mask[...]
    pl.semaphore_wait(barrier, count)

    def send_kv(i, n, r):
        p = peers[0][1] if r is None else r[1]
        rsem = own_sem if r is None else kv_sem.at[i, (quarters - r[0]) % quarters]
        remote(
            qkv.at[pl.ds(1, 2), :, lanes(p, i, n)], kv_s.at[0, :, my_rows, at(i, n)], a2a_send, rsem, (s, p)
        )

    def send_q(i, p):
        remote(qkv.at[0, :, lanes(p, i)], q_s.at[0, my_rows, at(i)], a2a_send, q_sem.at[i], (s, p))

    send_kv(0, hd, None)
    for r in peers[1:]:
        send_kv(0, 1, r)
    for k in (1, 2):
        @pl.when(has_q[k])
        def _():
            remote(mask_s.at[0], mask_s.at[3 - k], mk_send.at[k - 1], mk_recv.at[2 - k], q_dev[k])

    def forward_kv(i, g):
        where = pl.ds(pl.multiple_of(g * part, part), part)
        for k in (1, 2):
            @pl.when(has_kv[k])
            def _():
                ref = kv_s.at[0, :, where, at(i)]
                remote(ref, kv_s.at[3 - k, :, where, at(i)], z_send.at[k - 1], z_recv.at[i, 2 - k], kv_dev[k])

    own_part = pl.ds(pl.multiple_of(hi * part, part), part)
    wait(kv_s.at[0, :, own_part, :], own_sem)
    for i in range(hd):
        forward_kv(i, hi)
    for i in range(hd):
        if i > 0:
            for r in peers[1:]:
                send_kv(i, 1, r)
        for _, p in peers:
            send_q(i, p)

    m_s[...] = jnp.full_like(m_s, NEG)
    l_s[...] = jnp.zeros_like(l_s)
    acc_s[...] = jnp.zeros_like(acc_s)

    def update(i, qs, k, v, biases):
        q = q_s[qs, :, at(i)]
        m_old = m_s[qs, i]
        scores = []
        m_new = m_old
        for f, b in enumerate(biases):
            sc = lax.dot_general(
                k[f * tile:(f + 1) * tile], q, (((1,), (1,)), ((), ())), preferred_element_type=F32
            )
            top = jnp.max(sc, axis=0, keepdims=True)
            m_new = jnp.maximum(m_new, top if b is None else top + b)
            scores.append(sc)
        alpha = jnp.exp2((m_old - m_new) * C2)
        big = m_new * C2
        l_new = l_s[qs, i] * alpha
        acc = acc_s[qs, i] * alpha
        for f, b in enumerate(biases):
            sub = big if b is None else jnp.where(b < 0, -NEG, big)
            e = jnp.exp2(scores[f] * C2 - sub)
            l_new = l_new + jnp.sum(e, axis=0, keepdims=True)
            acc = acc + lax.dot_general(
                v[f * tile:(f + 1) * tile], e.astype(jnp.bfloat16), (((0,), (0,)), ((), ())),
                preferred_element_type=F32,
            )
        m_s[qs, i] = m_new
        l_s[qs, i] = l_new
        acc_s[qs, i] = acc

    def update_kv(i, qs, ks):
        update(i, qs, kv_s[ks, 0, :, at(i)], kv_s[ks, 1, :, at(i)], [bias_s[qs, ks, 0], bias_s[qs, ks, 1]])

    def make_bias(qs):
        lane = lax.broadcasted_iota(jnp.int32, (1, total), 1)
        for ks in range(3):
            for kf in range(2):
                picked = []
                for qf in range(2):
                    o = (kf - qf + 1) * 9 + (1, 0, 2)[ks] * 3 + (1, 2, 0)[qs]
                    picked.append(jnp.broadcast_to(mask_s[qs, qf:qf + 1, o:o + 1], (1, total)))
                chosen = jnp.where(lane < tile, picked[0], picked[1])
                bias_s[qs, ks, kf] = jnp.where(chosen > 0, 0.0, NEG).astype(F32)

    make_bias(0)
    wait(text_s, text_sem)
    for i in range(hd):
        for r in dict.fromkeys(r for r, _ in peers[1:]):
            back = (quarters - r) % quarters
            g = (hi + back) % quarters
            where = pl.ds(pl.multiple_of(g * part, part), part)
            wait(kv_s.at[0, :, where, at(i)], kv_sem.at[i, back])
            forward_kv(i, g)
        wait(q_s.at[0, :, at(i)], q_sem.at[i])
        for k in (1, 2):
            @pl.when(has_q[k])
            def _():
                remote(q_s.at[0, :, at(i)], q_s.at[3 - k, :, at(i)], x_send.at[k - 1], x_recv.at[i, 2 - k], q_dev[k])
        update(i, 0, text_s[0, :, at(i)], text_s[1, :, at(i)], [None] * (text_s.shape[1] // tile))
        update_kv(i, 0, 0)

    for k in (1, 2):
        @pl.when(has_q[k])
        def _():
            wait(mask_s.at[k], mk_recv.at[k - 1])
            make_bias(k)

        @pl.when(jnp.logical_not(has_q[k]))
        def _():
            orecv_s[k - 1] = jnp.zeros_like(orecv_s[k - 1])
            lrecv_s[k - 1] = jnp.full_like(lrecv_s[k - 1], NEG)
    for i in range(hd):
        for k in (1, 2):
            @pl.when(has_q[k])
            def _():
                wait(q_s.at[k, :, at(i)], x_recv.at[i, k - 1])
                update_kv(i, k, 0)

    def finish(i):
        parts = []
        for k in (1, 2):
            @pl.when(has_q[k])
            def _():
                wait(orecv_s.at[k - 1, i], o_recv.at[i, k - 1])
                wait(lrecv_s.at[k - 1, i], ls_recv.at[i, k - 1])

            parts.append((lrecv_s[k - 1, i, 0:1], orecv_s[k - 1, i].astype(F32)))
        l = l_s[0, i]
        lse = m_s[0, i] * C2 + jnp.log2(l)
        top = jnp.maximum(lse, jnp.maximum(parts[0][0], parts[1][0]))
        w = jnp.exp2(lse - top)
        w1, w2 = jnp.exp2(parts[0][0] - top), jnp.exp2(parts[1][0] - top)
        scale = 1.0 / (w + w1 + w2)
        o = acc_s[0, i] * (w * scale / l) + parts[0][1] * (w1 * scale) + parts[1][1] * (w2 * scale)
        ofin_s[:, at(i)] = o.T.astype(jnp.bfloat16)
        for _, p in peers:
            remote(
                ofin_s.at[pl.ds(pl.multiple_of(p * rows, rows), rows), at(i)], out.at[:, lanes(my, i)],
                out_send, out_sem, (s, p),
            )
        pltpu.make_async_copy(ofin_s.at[my_rows, at(i)], out.at[:, lanes(my, i)], out_sem).start()

    for i in range(hd):
        for k in (1, 2):
            @pl.when(has_kv[k])
            def _():
                wait(kv_s.at[k, :, :, at(i)], z_recv.at[i, k - 1])
                for qs in (1, 2, 0):
                    if qs == 0:
                        update_kv(i, 0, k)
                    else:
                        @pl.when(has_q[qs])
                        def _():
                            update_kv(i, qs, k)

        for k in (1, 2):
            @pl.when(has_q[k])
            def _():
                l = l_s[k, i]
                some = l > 0
                osend_s[k - 1, i] = (acc_s[k, i] * jnp.where(some, 1.0 / l, 0.0)).astype(jnp.bfloat16)
                lsend_s[k - 1, i] = jnp.broadcast_to(
                    jnp.where(some, m_s[k, i] * C2 + jnp.log2(l), NEG), lsend_s.shape[2:]
                )
                remote(osend_s.at[k - 1, i], orecv_s.at[2 - k, i], o_send.at[k - 1], o_recv.at[i, 2 - k], q_dev[k])
                remote(lsend_s.at[k - 1, i], lrecv_s.at[2 - k, i], ls_send.at[k - 1], ls_recv.at[i, 2 - k], q_dev[k])
        if i > 0:
            finish(i - 1)
    finish(hd - 1)

    less = total - rows
    wait(kv_s.at[0, :, pl.ds(0, less), :], a2a_send)
    wait(q_s.at[0, pl.ds(0, less), :], a2a_send)
    for k in (1, 2):
        @pl.when(has_kv[k])
        def _():
            wait(kv_s.at[0], z_send.at[k - 1])

        @pl.when(has_q[k])
        def _():
            wait(q_s.at[0], x_send.at[k - 1])
            wait(mask_s.at[0], mk_send.at[k - 1])
            wait(osend_s.at[k - 1], o_send.at[k - 1])
            wait(lsend_s.at[k - 1], ls_send.at[k - 1])
    wait(ofin_s.at[pl.ds(0, less), :], out_send)
    wait(out, out_sem)


def solution(mesh):
    nh = mesh.shape["head"]
    grid_rows = mesh.shape["seq"] // GW

    def on_device(qkv, text_kv, window_mask):
        _, rows, d = qkv.shape
        txt, width = text_kv.shape[1:]
        hd = width // HEAD_DIM
        total = rows * nh
        quarters = nh // CORES
        bf = jnp.bfloat16
        dma = pltpu.SemaphoreType.DMA
        return pl.pallas_call(
            functools.partial(kernel, grid_rows, nh, hd),
            out_shape=jax.ShapeDtypeStruct((rows, d), bf),
            in_specs=[
                pl.BlockSpec(memory_space=pl.ANY),
                pl.BlockSpec(memory_space=pl.ANY),
                pl.BlockSpec(memory_space=pltpu.VMEM),
            ],
            out_specs=pl.BlockSpec(memory_space=pltpu.VMEM),
            scratch_shapes=[
                pltpu.VMEM((3, total, width), bf),
                pltpu.VMEM((3, 2, total, width), bf),
                pltpu.VMEM((2, txt, width), bf),
                pltpu.VMEM((3, 8, 128), jnp.int32),
                pltpu.VMEM((3, 3, 2, 1, total), F32),
                pltpu.VMEM((3, hd, 1, total), F32),
                pltpu.VMEM((3, hd, 1, total), F32),
                pltpu.VMEM((3, hd, HEAD_DIM, total), F32),
                pltpu.VMEM((2, hd, HEAD_DIM, total), bf),
                pltpu.VMEM((2, hd, HEAD_DIM, total), bf),
                pltpu.VMEM((2, hd, 8, total), F32),
                pltpu.VMEM((2, hd, 8, total), F32),
                pltpu.VMEM((total, width), bf),
                dma, dma((hd, quarters)), dma((hd,)), dma, dma,
                dma((2,)), dma((hd, 2)), dma((2,)), dma((hd, 2)), dma((2,)), dma((2,)),
                dma((2,)), dma((hd, 2)), dma((2,)), dma((hd, 2)), dma, dma,
            ],
            compiler_params=pltpu.CompilerParams(
                collective_id=0, has_side_effects=True, vmem_limit_bytes=48 << 20
            ),
            cost_estimate=pl.CostEstimate(
                flops=4 * total * hd * HEAD_DIM * (9 * total + txt),
                bytes_accessed=8 * rows * d,
                transcendentals=total * hd * (9 * total + txt),
            ),
        )(qkv, text_kv, window_mask)

    return jax.shard_map(
        on_device, mesh=mesh,
        in_specs=(P(None, ("seq", "head"), None), P(None, None, "head"), P("seq", None)),
        out_specs=P(("seq", "head"), None), check_vma=False,
    )
```

```python
import functools
import math

import jax
import jax.numpy as jnp
from jax import lax
from jax.experimental import pallas as pl
from jax.experimental.pallas import tpu as pltpu
from jax.sharding import PartitionSpec as P

HEAD_DIM = 128
GW = 8
CORES = 2
MESH = pl.DeviceIdType.MESH
NEG = -1e30
C2 = math.log2(math.e) / math.sqrt(HEAD_DIM)
F32 = jnp.float32
MODES = (0, 0, 1)
PLAN = (
    ("y", "kv", 0), ("f", 0, 0), ("ys", "kv", 0), ("y", "q", 0), ("f", 0, 1), ("f", 0, 3), ("f", 0, 2),
    ("ys", "q", 0), ("y", "q", 2), ("q", 0), ("text", 0), ("c", 0, 0, 0), ("ys", "q", 2), ("y", "kv", 1),
    ("c", 0, 1, 0), ("c", 0, 2, 0), ("fs", 0), ("q", 2), ("qs", 2), ("ys", "kv", 1), ("y", "kv", 2), ("f", 1, 0),
    ("f", 1, 1), ("f", 1, 3), ("f", 1, 2), ("c", 0, 1, 1), ("c", 0, 1, 2), ("c", 0, 2, 1), ("c", 0, 2, 2), ("r", 0),
    ("c", 0, 0, 1), ("c", 0, 0, 2), ("text", 2), ("ys", "kv", 2), ("y", "q", 1), ("n", 0), ("f", 2, 0), ("f", 2, 1),
    ("f", 2, 3), ("f", 2, 2), ("c", 2, 0, 0), ("c", 2, 1, 0), ("c", 2, 2, 0), ("q", 1), ("text", 1), ("c", 1, 0, 0),
    ("c", 1, 1, 0), ("c", 1, 2, 0), ("c", 2, 1, 1), ("c", 2, 1, 2), ("c", 2, 2, 1), ("c", 2, 2, 2), ("r", 2),
    ("c", 2, 0, 1), ("c", 2, 0, 2), ("c", 1, 1, 1), ("c", 1, 1, 2), ("c", 1, 2, 1), ("c", 1, 2, 2), ("r", 1),
    ("c", 1, 0, 1), ("c", 1, 0, 2), ("n", 2), ("n", 1),
)


def kernel(
    grid_rows, nh, hd,
    qkv, text, mask, out,
    q_s, kv_s, text_s, mask_s, bias_s, m_s, l_s, acc_s, osend_s, orecv_s, lsend_s, lrecv_s, ofin_s,
    own_sem, kv_sem, q_sem, text_sem, a2a_send,
    kv_send, kv_recv, q_send, q_recv, mk_send, mk_recv, o_send, o_recv, ls_send, ls_recv, out_send, out_sem,
):
    s, my = lax.axis_index("seq"), lax.axis_index("head")
    row, col = s // GW, s % GW
    rows = qkv.shape[1]
    total = rows * nh
    tile = total // 2
    quarters = nh // CORES
    part = rows * CORES
    core, hi = my % CORES, my // CORES
    has = [[None, row > 0, row < grid_rows - 1], [None, col > 0, col < GW - 1]]
    dev = [[None, (s - GW, my), (s + GW, my)], [None, (s - 1, my), (s + 1, my)]]
    kv_axis = [MODES[i] for i in range(hd)]
    q_axis = [1 - MODES[i] for i in range(hd)]
    mate = hi * CORES + 1 - core
    far = [(r, ((hi + r) % quarters) * CORES + (core + o) % CORES) for r in range(1, quarters) for o in range(CORES)]
    peers = [(0, mate)] + sorted(far, key=lambda p: 2 * p[0] == quarters)
    my_rows = pl.ds(pl.multiple_of(my * rows, rows), rows)

    def lanes(h, i, n=1):
        return pl.ds(pl.multiple_of((h * hd + i) * HEAD_DIM, HEAD_DIM), n * HEAD_DIM)

    def at(i, n=1):
        return pl.ds(i * HEAD_DIM, n * HEAD_DIM)

    def remote(src, dst, ssem, rsem, device):
        pltpu.make_async_remote_copy(
            src_ref=src, dst_ref=dst, send_sem=ssem, recv_sem=rsem, device_id=device, device_id_type=MESH
        ).start()

    def wait(ref, sem):
        pltpu.make_async_copy(ref, ref, sem).wait()

    pltpu.make_async_copy(qkv.at[pl.ds(1, 2), :, lanes(my, 0, hd)], kv_s.at[0, :, my_rows, :], own_sem).start()
    for i in range(hd):
        pltpu.make_async_copy(qkv.at[0, :, lanes(my, i)], q_s.at[0, my_rows, at(i)], q_sem.at[i]).start()
    pltpu.make_async_copy(text, text_s, text_sem).start()

    barrier = pltpu.get_barrier_semaphore()
    count = len(peers)
    for _, p in peers:
        pl.semaphore_signal(barrier, inc=1, device_id=(s, p), device_id_type=MESH)
    for a in (0, 1):
        for k in (1, 2):
            count = count + has[a][k].astype(jnp.int32)

            @pl.when(has[a][k])
            def _():
                pl.semaphore_signal(barrier, inc=1, device_id=dev[a][k], device_id_type=MESH)

    m_s[...] = jnp.full_like(m_s, NEG)
    l_s[...] = jnp.zeros_like(l_s)
    acc_s[...] = jnp.zeros_like(acc_s)
    pl.semaphore_wait(barrier, count)

    remote(qkv.at[pl.ds(1, 2), :, lanes(mate, 0, hd)], kv_s.at[0, :, my_rows, :], a2a_send.at[2, 0], own_sem, (s, mate))

    def send(kind, i):
        for r, p in peers:
            if kind == 0:
                remote(qkv.at[0, :, lanes(p, i)], q_s.at[0, my_rows, at(i)], a2a_send.at[0, i], q_sem.at[i], (s, p))
            elif r > 0:
                remote(
                    qkv.at[pl.ds(1, 2), :, lanes(p, i)], kv_s.at[0, :, my_rows, at(i)],
                    a2a_send.at[1, i], kv_sem.at[i, quarters - r], (s, p),
                )

    def sent(kind, i):
        if kind == 0:
            wait(q_s.at[0, pl.ds(0, total - rows), at(i)], a2a_send.at[0, i])
        else:
            wait(kv_s.at[0, :, pl.ds(0, total - part), at(i)], a2a_send.at[1, i])

    def make_bias(mode, qs):
        which = 0 if qs == 0 else 1 + 2 * (1 - mode) + qs - 1
        lane = lax.broadcasted_iota(jnp.int32, (1, total), 1)
        for ks in range(3):
            for kf in range(2):
                picked = []
                for qf in range(2):
                    along_kv, along_q = (1, 0, 2)[ks], (1, 2, 0)[qs]
                    o = (kf - qf + 1) * 9 + (along_kv * 3 + along_q if mode == 0 else along_q * 3 + along_kv)
                    picked.append(jnp.broadcast_to(mask_s[which, qf:qf + 1, o:o + 1], (1, total)))
                chosen = jnp.where(lane < tile, picked[0], picked[1])
                bias_s[mode, qs, ks, kf] = jnp.where(chosen > 0, 0.0, NEG).astype(F32)

    def forward_kv(i, back):
        g = (hi + back) % quarters
        where = pl.ds(pl.multiple_of(g * part, part), part)
        if back > 0:
            wait(kv_s.at[0, :, where, at(i)], kv_sem.at[i, back])
        a = kv_axis[i]
        for k in (1, 2):
            @pl.when(has[a][k])
            def _():
                remote(
                    kv_s.at[0, :, where, at(i)], kv_s.at[3 - k, :, where, at(i)],
                    kv_send.at[i, k - 1], kv_recv.at[i, 2 - k], dev[a][k],
                )

    def forwarded_kv(i):
        for k in (1, 2):
            @pl.when(has[kv_axis[i]][k])
            def _():
                wait(kv_s.at[0, :, :, at(i)], kv_send.at[i, k - 1])

    def forward_q(i):
        wait(q_s.at[0, :, at(i)], q_sem.at[i])
        a = q_axis[i]
        for k in (1, 2):
            @pl.when(has[a][k])
            def _():
                remote(q_s.at[0, :, at(i)], q_s.at[3 - k, :, at(i)], q_send.at[i, k - 1], q_recv.at[i, 2 - k], dev[a][k])

    def forwarded_q(i):
        for k in (1, 2):
            @pl.when(has[q_axis[i]][k])
            def _():
                wait(q_s.at[0, :, at(i)], q_send.at[i, k - 1])

    def update(i, qs, k, v, biases):
        q = q_s[qs, :, at(i)]
        m_old = m_s[qs, i]
        scores = []
        m_new = m_old
        for f, b in enumerate(biases):
            sc = lax.dot_general(
                k[f * tile:(f + 1) * tile], q, (((1,), (1,)), ((), ())), preferred_element_type=F32
            )
            top = jnp.max(sc, axis=0, keepdims=True)
            m_new = jnp.maximum(m_new, top if b is None else top + b)
            scores.append(sc)
        alpha = jnp.exp2((m_old - m_new) * C2)
        big = m_new * C2
        l_new = l_s[qs, i] * alpha
        acc = acc_s[qs, i] * alpha
        for f, b in enumerate(biases):
            sub = big if b is None else jnp.where(b < 0, -NEG, big)
            e = jnp.exp2(scores[f] * C2 - sub)
            l_new = l_new + jnp.sum(e, axis=0, keepdims=True)
            acc = acc + lax.dot_general(
                v[f * tile:(f + 1) * tile], e.astype(jnp.bfloat16), (((0,), (0,)), ((), ())),
                preferred_element_type=F32,
            )
        m_s[qs, i] = m_new
        l_s[qs, i] = l_new
        acc_s[qs, i] = acc

    landed = set()

    def block(i, qs, ks):
        need_q, need_kv = qs and ("q", i, qs) not in landed, ks and ("kv", i, ks) not in landed
        if need_q:
            landed.add(("q", i, qs))

            @pl.when(has[q_axis[i]][qs])
            def _():
                wait(q_s.at[qs, :, at(i)], q_recv.at[i, qs - 1])
        if need_kv:
            landed.add(("kv", i, ks))

            @pl.when(has[kv_axis[i]][ks])
            def _():
                wait(kv_s.at[ks, :, :, at(i)], kv_recv.at[i, ks - 1])

        def go():
            update(
                i, qs, kv_s[ks, 0, :, at(i)], kv_s[ks, 1, :, at(i)],
                [bias_s[MODES[i], qs, ks, 0], bias_s[MODES[i], qs, ks, 1]],
            )

        guards = ([has[q_axis[i]][qs]] if qs else []) + ([has[kv_axis[i]][ks]] if ks else [])
        if guards:
            pl.when(functools.reduce(jnp.logical_and, guards))(go)
        else:
            go()

    def text_block(i):
        update(i, 0, text_s[0, :, at(i)], text_s[1, :, at(i)], [None] * (text_s.shape[1] // tile))

    def give_back(i):
        a = q_axis[i]
        for k in (1, 2):
            @pl.when(has[a][k])
            def _():
                l = l_s[k, i]
                some = l > 0
                osend_s[k - 1, i] = (acc_s[k, i] * jnp.where(some, 1.0 / l, 0.0)).astype(jnp.bfloat16)
                lsend_s[k - 1, i] = jnp.broadcast_to(
                    jnp.where(some, m_s[k, i] * C2 + jnp.log2(l), NEG), lsend_s.shape[2:]
                )
                remote(osend_s.at[k - 1, i], orecv_s.at[2 - k, i], o_send.at[i, k - 1], o_recv.at[i, 2 - k], dev[a][k])
                remote(lsend_s.at[k - 1, i], lrecv_s.at[2 - k, i], ls_send.at[i, k - 1], ls_recv.at[i, 2 - k], dev[a][k])

    def finish(i):
        a = q_axis[i]
        parts = []
        for k in (1, 2):
            @pl.when(has[a][k])
            def _():
                wait(orecv_s.at[k - 1, i], o_recv.at[i, k - 1])
                wait(lrecv_s.at[k - 1, i], ls_recv.at[i, k - 1])

            @pl.when(jnp.logical_not(has[a][k]))
            def _():
                orecv_s[k - 1, i] = jnp.zeros_like(orecv_s[k - 1, i])
                lrecv_s[k - 1, i] = jnp.full_like(lrecv_s[k - 1, i], NEG)

            parts.append((lrecv_s[k - 1, i, 0:1], orecv_s[k - 1, i].astype(F32)))
        l = l_s[0, i]
        lse = m_s[0, i] * C2 + jnp.log2(l)
        top = jnp.maximum(lse, jnp.maximum(parts[0][0], parts[1][0]))
        w = jnp.exp2(lse - top)
        w1, w2 = jnp.exp2(parts[0][0] - top), jnp.exp2(parts[1][0] - top)
        scale = 1.0 / (w + w1 + w2)
        o = acc_s[0, i] * (w * scale / l) + parts[0][1] * (w1 * scale) + parts[1][1] * (w2 * scale)
        ofin_s[:, at(i)] = o.T.astype(jnp.bfloat16)
        for _, p in peers:
            remote(
                ofin_s.at[pl.ds(pl.multiple_of(p * rows, rows), rows), at(i)], out.at[:, lanes(my, i)],
                out_send, out_sem, (s, p),
            )
        pltpu.make_async_copy(ofin_s.at[my_rows, at(i)], out.at[:, lanes(my, i)], out_sem).start()

    def masks():
        mask_s[0] = jnp.zeros_like(mask_s[0])
        mask_s[0, 0:2, 0:27] = mask[...]
        for a in (0, 1):
            for k in (1, 2):
                @pl.when(has[a][k])
                def _():
                    remote(
                        mask_s.at[0], mask_s.at[1 + 2 * a + 2 - k], mk_send.at[a, k - 1], mk_recv.at[a, 2 - k], dev[a][k]
                    )

    def biases():
        for mode in sorted(set(MODES)):
            make_bias(mode, 0)
            for k in (1, 2):
                @pl.when(has[1 - mode][k])
                def _():
                    wait(mask_s.at[1 + 2 * (1 - mode) + k - 1], mk_recv.at[1 - mode, k - 1])
                    make_bias(mode, k)

    first = True
    kinds = {"q": 0, "kv": 1}
    for op, *rest in PLAN:
        if op == "y":
            send(kinds[rest[0]], rest[1])
        elif op == "ys":
            sent(kinds[rest[0]], rest[1])
        elif op == "f":
            if first:
                first = False
                own_part = pl.ds(pl.multiple_of(hi * part, part), part)
                wait(kv_s.at[0, :, own_part, :], own_sem)
                forward_kv(*rest)
                masks()
                biases()
                wait(text_s, text_sem)
            else:
                forward_kv(*rest)
        elif op == "fs":
            forwarded_kv(rest[0])
        elif op == "q":
            forward_q(rest[0])
        elif op == "qs":
            forwarded_q(rest[0])
        elif op == "text":
            text_block(rest[0])
        elif op == "c":
            block(*rest)
        elif op == "r":
            give_back(rest[0])
        elif op == "n":
            finish(rest[0])

    wait(kv_s.at[0, :, pl.ds(0, rows), :], a2a_send.at[2, 0])
    for i in range(hd):
        for kind, name in ((0, "q"), (1, "kv")):
            if ("ys", name, i) not in PLAN:
                sent(kind, i)
        if ("fs", i) not in PLAN:
            forwarded_kv(i)
        if ("qs", i) not in PLAN:
            forwarded_q(i)
        for k in (1, 2):
            @pl.when(has[q_axis[i]][k])
            def _():
                wait(osend_s.at[k - 1, i], o_send.at[i, k - 1])
                wait(lsend_s.at[k - 1, i], ls_send.at[i, k - 1])
    for a in (0, 1):
        for k in (1, 2):
            @pl.when(has[a][k])
            def _():
                wait(mask_s.at[0], mk_send.at[a, k - 1])
                if 1 - a not in MODES:
                    wait(mask_s.at[1 + 2 * a + k - 1], mk_recv.at[a, k - 1])
    wait(ofin_s.at[pl.ds(0, total - rows), :], out_send)
    wait(out, out_sem)


def solution(mesh):
    nh = mesh.shape["head"]
    grid_rows = mesh.shape["seq"] // GW

    def on_device(qkv, text_kv, window_mask):
        _, rows, d = qkv.shape
        txt, width = text_kv.shape[1:]
        hd = width // HEAD_DIM
        total = rows * nh
        quarters = nh // CORES
        bf = jnp.bfloat16
        dma = pltpu.SemaphoreType.DMA
        return pl.pallas_call(
            functools.partial(kernel, grid_rows, nh, hd),
            out_shape=jax.ShapeDtypeStruct((rows, d), bf),
            in_specs=[
                pl.BlockSpec(memory_space=pl.ANY),
                pl.BlockSpec(memory_space=pl.ANY),
                pl.BlockSpec(memory_space=pltpu.VMEM),
            ],
            out_specs=pl.BlockSpec(memory_space=pltpu.VMEM),
            scratch_shapes=[
                pltpu.VMEM((3, total, width), bf),
                pltpu.VMEM((3, 2, total, width), bf),
                pltpu.VMEM((2, txt, width), bf),
                pltpu.VMEM((5, 8, 128), jnp.int32),
                pltpu.VMEM((2, 3, 3, 2, 1, total), F32),
                pltpu.VMEM((3, hd, 1, total), F32),
                pltpu.VMEM((3, hd, 1, total), F32),
                pltpu.VMEM((3, hd, HEAD_DIM, total), F32),
                pltpu.VMEM((2, hd, HEAD_DIM, total), bf),
                pltpu.VMEM((2, hd, HEAD_DIM, total), bf),
                pltpu.VMEM((2, hd, 8, total), F32),
                pltpu.VMEM((2, hd, 8, total), F32),
                pltpu.VMEM((total, width), bf),
                dma, dma((hd, quarters)), dma((hd,)), dma, dma((3, hd)),
                dma((hd, 2)), dma((hd, 2)), dma((hd, 2)), dma((hd, 2)), dma((2, 2)), dma((2, 2)),
                dma((hd, 2)), dma((hd, 2)), dma((hd, 2)), dma((hd, 2)), dma, dma,
            ],
            compiler_params=pltpu.CompilerParams(
                collective_id=0, has_side_effects=True, vmem_limit_bytes=60 << 20
            ),
            cost_estimate=pl.CostEstimate(
                flops=4 * total * hd * HEAD_DIM * (9 * total + txt),
                bytes_accessed=8 * rows * d,
                transcendentals=total * hd * (9 * total + txt),
            ),
        )(qkv, text_kv, window_mask)

    return jax.shard_map(
        on_device, mesh=mesh,
        in_specs=(P(None, ("seq", "head"), None), P(None, None, "head"), P("seq", None)),
        out_specs=P(("seq", "head"), None), check_vma=False,
    )
```

```python
import functools
import math

import jax
import jax.numpy as jnp
from jax import lax
from jax.experimental import pallas as pl
from jax.experimental.pallas import tpu as pltpu
from jax.sharding import PartitionSpec as P

HEAD_DIM = 128
GW = 8
CORES = 2
MESH = pl.DeviceIdType.MESH
NEG = -1e30
C2 = math.log2(math.e) / math.sqrt(HEAD_DIM)
F32 = jnp.float32
MODES = (0, 0, 0)
EDGE = GW // 2 - 1
ROUTES = {1: (0, 7)}
PLAN = (
    ("y", "kv", 0), ("f", 0, 0), ("y", "q", 0), ("y", "kv", 1), ("y", "q", 1), ("y", "kv", 2), ("y", "q", 2),
    ("f", 0, 1), ("f", 0, 3), ("f", 0, 2), ("q", 0), ("f", 1, 0), ("f", 1, 1), ("f", 1, 3), ("f", 1, 2), ("q", 1),
    ("rq", 1), ("text", 0), ("c", 0, 0, 0), ("c", 0, 1, 0), ("c", 0, 2, 0), ("fs", 0), ("f", 2, 0), ("f", 2, 1),
    ("f", 2, 3), ("f", 2, 2), ("q", 2), ("c", 0, 1, 1), ("c", 0, 2, 1), ("c", 0, 1, 2), ("c", 0, 2, 2), ("r", 0),
    ("c", 0, 0, 1), ("c", 0, 0, 2), ("text", 1), ("c", 1, 0, 0), ("c", 1, 1, 0), ("c", 1, 2, 0), ("c", 1, 1, 1),
    ("c", 1, 2, 1), ("c", 1, 1, 2), ("c", 1, 2, 2), ("r", 1), ("ro", 1), ("n", 0), ("text", 2), ("c", 2, 0, 0),
    ("c", 2, 1, 0), ("c", 2, 2, 0), ("c", 1, 0, 1), ("c", 1, 0, 2), ("c", 2, 1, 1), ("c", 2, 2, 1), ("c", 2, 1, 2),
    ("c", 2, 2, 2), ("r", 2), ("c", 2, 0, 1), ("c", 2, 0, 2), ("n", 1), ("n", 2),
)


def kernel(
    grid_rows, nh, hd,
    qkv, text, mask, out,
    q_s, kv_s, text_s, mask_s, mask_t, bias_s, m_s, l_s, acc_s, osend_s, orecv_s, lsend_s, lrecv_s, ofin_s, relay_q, relay_o,
    kv_sem, q_sem, text_sem, a2a_send,
    kv_send, kv_recv, q_send, q_recv, mk_send, mk_recv, o_send, o_recv, ls_send, ls_recv, out_send, out_sem, relay_sem,
):
    s, my = lax.axis_index("seq"), lax.axis_index("head")
    rows = qkv.shape[1]
    total = rows * nh
    tile = total // 2
    quarters = nh // CORES
    part = rows * CORES
    core, hi = my % CORES, my // CORES
    half = grid_rows * GW // 2
    lo, rest_s = s // half, s % half
    c = core * half + rest_s
    group = hi * 2 + lo
    row, col = c // GW, c % GW
    home = core == lo

    def holder(column):
        return (lo * half + column % half, hi * CORES + column // half)

    has = [[None, row > 0, row < grid_rows - 1], [None, col > 0, col < GW - 1]]
    dev = [[None, holder(c - GW), holder(c + GW)], [None, holder(c - 1), holder(c + 1)]]
    on_edge = [None, col == EDGE + 1, col == EDGE]

    def relays(i):
        return [(ROUTES[i][0], EDGE + 1, 1, EDGE), (ROUTES[i][1], EDGE, 2, EDGE + 1)] if i in ROUTES else []

    kv_axis = [MODES[i] for i in range(hd)]
    q_axis = [1 - MODES[i] for i in range(hd)]
    steps = [0] + sorted(range(1, quarters), key=lambda t: 2 * t == quarters)
    goes = []
    for t in steps:
        to = lax.rem(hi + quarters - t, quarters)
        for l in (lo, 1 - lo):
            goes.append((t, (l * half + rest_s, to * CORES + lo), to * 2 + l, t == 0 and l is lo))
    owners = [(core * half + rest_s, j) for j in range(nh)]
    my_rows = pl.ds(pl.multiple_of(my * rows, rows), rows)

    def lanes(h, i, n=1):
        return pl.ds(pl.multiple_of((h * hd + i) * HEAD_DIM, HEAD_DIM), n * HEAD_DIM)

    def at(i, n=1):
        return pl.ds(i * HEAD_DIM, n * HEAD_DIM)

    def remote(src, dst, ssem, rsem, device):
        pltpu.make_async_remote_copy(
            src_ref=src, dst_ref=dst, send_sem=ssem, recv_sem=rsem, device_id=device, device_id_type=MESH
        ).start()

    def wait(ref, sem):
        pltpu.make_async_copy(ref, ref, sem).wait()

    mate = (s, hi * CORES + 1 - core)
    across = ((1 - lo) * half + rest_s, my)

    barrier = pltpu.get_barrier_semaphore()
    count = len(goes) + quarters - home.astype(jnp.int32)
    for _, to, _, maybe in goes:
        if maybe:
            @pl.when(jnp.logical_not(home))
            def _():
                pl.semaphore_signal(barrier, inc=1, device_id=to, device_id_type=MESH)
        else:
            pl.semaphore_signal(barrier, inc=1, device_id=to, device_id_type=MESH)
    for t in range(quarters):
        pl.semaphore_signal(
            barrier, inc=1, device_id=(core * half + rest_s, t * CORES + 1 - lo), device_id_type=MESH
        )
    for a in (0, 1):
        for k in (1, 2):
            count = count + has[a][k].astype(jnp.int32)

            @pl.when(has[a][k])
            def _():
                pl.semaphore_signal(barrier, inc=1, device_id=dev[a][k], device_id_type=MESH)

    for i in ROUTES:
        for at_col, to_col, slot, from_col in relays(i):
            count = count + (col == from_col).astype(jnp.int32) + (col == at_col).astype(jnp.int32)

            @pl.when(col == at_col)
            def _():
                pl.semaphore_signal(barrier, inc=1, device_id=holder(c - at_col + from_col), device_id_type=MESH)

            @pl.when(col == to_col)
            def _():
                pl.semaphore_signal(barrier, inc=1, device_id=holder(c - to_col + at_col), device_id_type=MESH)

    @pl.when(home)
    def _():
        pltpu.make_async_copy(text, text_s, text_sem).start()

    mask_s[0] = jnp.zeros_like(mask_s[0])

    @pl.when(home)
    def _():
        mask_s[0, 0:2, 0:27] = mask[...]

    m_s[...] = jnp.full_like(m_s, NEG)
    l_s[...] = jnp.zeros_like(l_s)
    acc_s[...] = jnp.zeros_like(acc_s)
    pl.semaphore_wait(barrier, count)

    @pl.when(home)
    def _():
        mask_t[0] = mask_s[0]
        remote(mask_t.at[0], mask_t.at[1], mk_send.at[2, 0], mk_recv.at[2, 0], across)
        remote(text, text_s, mk_send.at[2, 1], text_sem, mate)

    def send(kind, i):
        for t, to, g, maybe in goes:
            if kind == 0:
                src, dst = qkv.at[0, :, lanes(g, i)], q_s.at[0, my_rows, at(i)]
                ssem, rsem = a2a_send.at[0, i], q_sem.at[i]
            else:
                src, dst = qkv.at[pl.ds(1, 2), :, lanes(g, i)], kv_s.at[0, :, my_rows, at(i)]
                ssem, rsem = a2a_send.at[1, i], kv_sem.at[i, t]
            if maybe:
                @pl.when(home)
                def _():
                    pltpu.make_async_copy(src, dst, rsem).start()

                @pl.when(jnp.logical_not(home))
                def _():
                    remote(src, dst, ssem, rsem, to)
            else:
                remote(src, dst, ssem, rsem, to)

    def sent(kind, i):
        sem = a2a_send.at[kind, i]
        block_of = (lambda n: q_s.at[0, pl.ds(0, n), at(i)]) if kind == 0 else (lambda n: kv_s.at[0, :, pl.ds(0, n), at(i)])

        @pl.when(home)
        def _():
            wait(block_of(total - rows), sem)

        @pl.when(jnp.logical_not(home))
        def _():
            wait(block_of(total), sem)

    def make_bias(mode, qs):
        which = 0 if qs == 0 else 1 + 2 * (1 - mode) + qs - 1
        lane = lax.broadcasted_iota(jnp.int32, (1, total), 1)
        for ks in range(3):
            for kf in range(2):
                picked = []
                for qf in range(2):
                    along_kv, along_q = (1, 0, 2)[ks], (1, 2, 0)[qs]
                    o = (kf - qf + 1) * 9 + (along_kv * 3 + along_q if mode == 0 else along_q * 3 + along_kv)
                    picked.append(jnp.broadcast_to(mask_s[which, qf:qf + 1, o:o + 1], (1, total)))
                chosen = jnp.where(lane < tile, picked[0], picked[1])
                bias_s[mode, qs, ks, kf] = jnp.where(chosen > 0, 0.0, NEG).astype(F32)

    def forward_kv(i, back):
        g = (hi + back) % quarters
        where = pl.ds(pl.multiple_of(g * part, part), part)
        wait(kv_s.at[0, :, where, at(i)], kv_sem.at[i, back])
        a = kv_axis[i]
        for k in (1, 2):
            @pl.when(has[a][k])
            def _():
                remote(
                    kv_s.at[0, :, where, at(i)], kv_s.at[3 - k, :, where, at(i)],
                    kv_send.at[i, k - 1], kv_recv.at[i, 2 - k], dev[a][k],
                )

    def forwarded_kv(i):
        for k in (1, 2):
            @pl.when(has[kv_axis[i]][k])
            def _():
                wait(kv_s.at[0, :, :, at(i)], kv_send.at[i, k - 1])

    def forward_q(i):
        wait(q_s.at[0, :, at(i)], q_sem.at[i])
        a = q_axis[i]
        for k in (1, 2):
            src, ssem = q_s.at[0, :, at(i)], q_send.at[i, k - 1]

            @pl.when(jnp.logical_and(has[a][k], jnp.logical_not(on_edge[k])) if i in ROUTES else has[a][k])
            def _():
                remote(src, q_s.at[3 - k, :, at(i)], ssem, q_recv.at[i, 2 - k], dev[a][k])

        for at_col, to_col, slot, from_col in relays(i):
            @pl.when(col == from_col)
            def _():
                remote(
                    q_s.at[0, :, at(i)], relay_q, q_send.at[i, 2 - slot], relay_sem.at[0], holder(c - from_col + at_col)
                )

    def pass_q(i):
        for at_col, to_col, slot, from_col in relays(i):
            @pl.when(col == at_col)
            def _():
                wait(relay_q, relay_sem.at[0])
                remote(
                    relay_q, q_s.at[slot, :, at(i)], relay_sem.at[1], q_recv.at[i, slot - 1], holder(c - at_col + to_col)
                )

    def pass_o(i):
        for at_col, to_col, slot, from_col in relays(i):
            @pl.when(col == at_col)
            def _():
                wait(relay_o, relay_sem.at[2])
                remote(
                    relay_o, orecv_s.at[slot - 1, i], relay_sem.at[3], o_recv.at[i, slot - 1], holder(c - at_col + to_col)
                )

    def forwarded_q(i):
        for k in (1, 2):
            @pl.when(has[q_axis[i]][k])
            def _():
                wait(q_s.at[0, :, at(i)], q_send.at[i, k - 1])

    def update(i, qs, k, v, biases):
        q = q_s[qs, :, at(i)]
        m_old = m_s[qs, i]
        scores = []
        m_new = m_old
        for f, b in enumerate(biases):
            sc = lax.dot_general(
                k[f * tile:(f + 1) * tile], q, (((1,), (1,)), ((), ())), preferred_element_type=F32
            )
            top = jnp.max(sc, axis=0, keepdims=True)
            m_new = jnp.maximum(m_new, top if b is None else top + b)
            scores.append(sc)
        alpha = jnp.exp2((m_old - m_new) * C2)
        big = m_new * C2
        l_new = l_s[qs, i] * alpha
        acc = acc_s[qs, i] * alpha
        for f, b in enumerate(biases):
            sub = big if b is None else jnp.where(b < 0, -NEG, big)
            e = jnp.exp2(scores[f] * C2 - sub)
            l_new = l_new + jnp.sum(e, axis=0, keepdims=True)
            acc = acc + lax.dot_general(
                v[f * tile:(f + 1) * tile], e.astype(jnp.bfloat16), (((0,), (0,)), ((), ())),
                preferred_element_type=F32,
            )
        m_s[qs, i] = m_new
        l_s[qs, i] = l_new
        acc_s[qs, i] = acc

    landed = set()

    def block(i, qs, ks):
        need_q, need_kv = qs and ("q", i, qs) not in landed, ks and ("kv", i, ks) not in landed
        if need_q:
            landed.add(("q", i, qs))

            @pl.when(has[q_axis[i]][qs])
            def _():
                wait(q_s.at[qs, :, at(i)], q_recv.at[i, qs - 1])
        if need_kv:
            landed.add(("kv", i, ks))

            @pl.when(has[kv_axis[i]][ks])
            def _():
                wait(kv_s.at[ks, :, :, at(i)], kv_recv.at[i, ks - 1])

        def go():
            update(
                i, qs, kv_s[ks, 0, :, at(i)], kv_s[ks, 1, :, at(i)],
                [bias_s[MODES[i], qs, ks, 0], bias_s[MODES[i], qs, ks, 1]],
            )

        guards = ([has[q_axis[i]][qs]] if qs else []) + ([has[kv_axis[i]][ks]] if ks else [])
        if guards:
            pl.when(functools.reduce(jnp.logical_and, guards))(go)
        else:
            go()

    def text_block(i):
        update(i, 0, text_s[0, :, at(i)], text_s[1, :, at(i)], [None] * (text_s.shape[1] // tile))

    def remote_o(i, k):
        @pl.when(jnp.logical_not(on_edge[k]) if i in ROUTES else has[1][k])
        def _():
            remote(
                osend_s.at[k - 1, i], orecv_s.at[2 - k, i], o_send.at[i, k - 1], o_recv.at[i, 2 - k], dev[1][k]
            )

    def give_back(i):
        a = q_axis[i]
        for k in (1, 2):
            @pl.when(has[a][k])
            def _():
                l = l_s[k, i]
                some = l > 0
                osend_s[k - 1, i] = (acc_s[k, i] * jnp.where(some, 1.0 / l, 0.0)).astype(jnp.bfloat16)
                lsend_s[k - 1, i] = jnp.broadcast_to(
                    jnp.where(some, m_s[k, i] * C2 + jnp.log2(l), NEG), lsend_s.shape[2:]
                )
                remote_o(i, k)
                remote(lsend_s.at[k - 1, i], lrecv_s.at[2 - k, i], ls_send.at[i, k - 1], ls_recv.at[i, 2 - k], dev[a][k])

        for at_col, to_col, slot, from_col in relays(i):
            @pl.when(col == from_col)
            def _():
                remote(
                    osend_s.at[2 - slot, i], relay_o, o_send.at[i, 2 - slot], relay_sem.at[2],
                    holder(c - from_col + at_col),
                )

    def finish(i):
        a = q_axis[i]
        parts = []
        for k in (1, 2):
            @pl.when(has[a][k])
            def _():
                wait(orecv_s.at[k - 1, i], o_recv.at[i, k - 1])
                wait(lrecv_s.at[k - 1, i], ls_recv.at[i, k - 1])

            @pl.when(jnp.logical_not(has[a][k]))
            def _():
                orecv_s[k - 1, i] = jnp.zeros_like(orecv_s[k - 1, i])
                lrecv_s[k - 1, i] = jnp.full_like(lrecv_s[k - 1, i], NEG)

            parts.append((lrecv_s[k - 1, i, 0:1], orecv_s[k - 1, i].astype(F32)))
        l = l_s[0, i]
        lse = m_s[0, i] * C2 + jnp.log2(l)
        top = jnp.maximum(lse, jnp.maximum(parts[0][0], parts[1][0]))
        w = jnp.exp2(lse - top)
        w1, w2 = jnp.exp2(parts[0][0] - top), jnp.exp2(parts[1][0] - top)
        scale = 1.0 / (w + w1 + w2)
        o = acc_s[0, i] * (w * scale / l) + parts[0][1] * (w1 * scale) + parts[1][1] * (w2 * scale)
        ofin_s[:, at(i)] = o.T.astype(jnp.bfloat16)
        for j, to in enumerate(owners):
            src, dst = ofin_s.at[pl.ds(j * rows, rows), at(i)], out.at[:, lanes(group, i)]
            mine = jnp.logical_and(home, my == j)

            @pl.when(mine)
            def _():
                pltpu.make_async_copy(src, dst, out_sem).start()

            @pl.when(jnp.logical_not(mine))
            def _():
                remote(src, dst, out_send, out_sem, to)

    def masks():
        @pl.when(jnp.logical_not(home))
        def _():
            wait(mask_t.at[1], mk_recv.at[2, 0])
            mask_s[0] = mask_t[1]

        for a in (0, 1):
            for k in (1, 2):
                @pl.when(has[a][k])
                def _():
                    remote(
                        mask_s.at[0], mask_s.at[1 + 2 * a + 2 - k], mk_send.at[a, k - 1], mk_recv.at[a, 2 - k], dev[a][k]
                    )

    def biases():
        for mode in sorted(set(MODES)):
            make_bias(mode, 0)
            for k in (1, 2):
                @pl.when(has[1 - mode][k])
                def _():
                    wait(mask_s.at[1 + 2 * (1 - mode) + k - 1], mk_recv.at[1 - mode, k - 1])
                    make_bias(mode, k)

    first = True
    kinds = {"q": 0, "kv": 1}
    for op, *rest in PLAN:
        if op == "y":
            send(kinds[rest[0]], rest[1])
        elif op == "ys":
            sent(kinds[rest[0]], rest[1])
        elif op == "f":
            if first:
                first = False
                forward_kv(*rest)
                masks()
                biases()
                wait(text_s, text_sem)
            else:
                forward_kv(*rest)
        elif op == "fs":
            forwarded_kv(rest[0])
        elif op == "q":
            forward_q(rest[0])
        elif op == "qs":
            forwarded_q(rest[0])
        elif op == "text":
            text_block(rest[0])
        elif op == "c":
            block(*rest)
        elif op == "r":
            give_back(rest[0])
        elif op == "rq":
            pass_q(rest[0])
        elif op == "ro":
            pass_o(rest[0])
        elif op == "n":
            finish(rest[0])

    @pl.when(home)
    def _():
        wait(mask_t.at[0], mk_send.at[2, 0])
        wait(text_s, mk_send.at[2, 1])
        wait(ofin_s.at[pl.ds(0, total - rows), :], out_send)

    @pl.when(jnp.logical_not(home))
    def _():
        wait(ofin_s, out_send)

    for i in ROUTES:
        for at_col, to_col, slot, from_col in relays(i):
            @pl.when(col == at_col)
            def _():
                wait(relay_q, relay_sem.at[1])
                wait(relay_o, relay_sem.at[3])

    for i in range(hd):
        for kind, name in ((0, "q"), (1, "kv")):
            if ("ys", name, i) not in PLAN:
                sent(kind, i)
        if ("fs", i) not in PLAN:
            forwarded_kv(i)
        if ("qs", i) not in PLAN:
            forwarded_q(i)
        for k in (1, 2):
            @pl.when(has[q_axis[i]][k])
            def _():
                wait(osend_s.at[k - 1, i], o_send.at[i, k - 1])
                wait(lsend_s.at[k - 1, i], ls_send.at[i, k - 1])
    for a in (0, 1):
        for k in (1, 2):
            @pl.when(has[a][k])
            def _():
                wait(mask_s.at[0], mk_send.at[a, k - 1])
                if 1 - a not in MODES:
                    wait(mask_s.at[1 + 2 * a + k - 1], mk_recv.at[a, k - 1])
    wait(out, out_sem)


def solution(mesh):
    nh = mesh.shape["head"]
    grid_rows = mesh.shape["seq"] // GW

    def on_device(qkv, text_kv, window_mask):
        _, rows, d = qkv.shape
        txt, width = text_kv.shape[1:]
        hd = width // HEAD_DIM
        total = rows * nh
        quarters = nh // CORES
        bf = jnp.bfloat16
        dma = pltpu.SemaphoreType.DMA
        return pl.pallas_call(
            functools.partial(kernel, grid_rows, nh, hd),
            out_shape=jax.ShapeDtypeStruct((rows, d), bf),
            in_specs=[
                pl.BlockSpec(memory_space=pl.ANY),
                pl.BlockSpec(memory_space=pl.ANY),
                pl.BlockSpec(memory_space=pltpu.VMEM),
            ],
            out_specs=pl.BlockSpec(memory_space=pltpu.VMEM),
            scratch_shapes=[
                pltpu.VMEM((3, total, width), bf),
                pltpu.VMEM((3, 2, total, width), bf),
                pltpu.VMEM((2, txt, width), bf),
                pltpu.VMEM((5, 8, 128), jnp.int32),
                pltpu.VMEM((2, 8, 128), jnp.int32),
                pltpu.VMEM((2, 3, 3, 2, 1, total), F32),
                pltpu.VMEM((3, hd, 1, total), F32),
                pltpu.VMEM((3, hd, 1, total), F32),
                pltpu.VMEM((3, hd, HEAD_DIM, total), F32),
                pltpu.VMEM((2, hd, HEAD_DIM, total), bf),
                pltpu.VMEM((2, hd, HEAD_DIM, total), bf),
                pltpu.VMEM((2, hd, 8, total), F32),
                pltpu.VMEM((2, hd, 8, total), F32),
                pltpu.VMEM((total, width), bf),
                pltpu.VMEM((total, HEAD_DIM), bf),
                pltpu.VMEM((HEAD_DIM, total), bf),
                dma((hd, quarters)), dma((hd,)), dma, dma((2, hd)),
                dma((hd, 2)), dma((hd, 2)), dma((hd, 2)), dma((hd, 2)), dma((3, 2)), dma((3, 2)),
                dma((hd, 2)), dma((hd, 2)), dma((hd, 2)), dma((hd, 2)), dma, dma, dma((4,)),
            ],
            compiler_params=pltpu.CompilerParams(
                collective_id=0, has_side_effects=True, vmem_limit_bytes=60 << 20
            ),
            cost_estimate=pl.CostEstimate(
                flops=4 * total * hd * HEAD_DIM * (9 * total + txt),
                bytes_accessed=8 * rows * d,
                transcendentals=total * hd * (9 * total + txt),
            ),
        )(qkv, text_kv, window_mask)

    return jax.shard_map(
        on_device, mesh=mesh,
        in_specs=(P(None, ("seq", "head"), None), P(None, None, "head"), P("seq", None)),
        out_specs=P(("seq", "head"), None), check_vma=False,
    )
```

```python
import functools
import math

import jax
import jax.numpy as jnp
from jax import lax
from jax.experimental import pallas as pl
from jax.experimental.pallas import tpu as pltpu
from jax.sharding import PartitionSpec as P

HEAD_DIM = 128
GW = 8
CORES = 2
MESH = pl.DeviceIdType.MESH
NEG = -1e30
C2 = math.log2(math.e) / math.sqrt(HEAD_DIM)
F32 = jnp.float32
MODES = (0, 0, 0)
EDGE = GW // 2 - 1
RELAYS = (0, 7)
RELAY_Q = (0, 1)
RELAY_O = (0,)
PLAN = (
    ("y", "kv", 0), ("f", 0, 0), ("y", "q", 0), ("y", "kv", 1), ("y", "q", 1), ("y", "kv", 2), ("y", "q", 2),
    ("f", 0, 1), ("f", 0, 3), ("f", 0, 2), ("q", 0), ("f", 1, 0), ("f", 1, 1), ("f", 1, 3), ("f", 1, 2), ("rq", 0),
    ("q", 1), ("f", 2, 0), ("own", 0), ("f", 2, 1), ("f", 2, 3), ("f", 2, 2), ("q", 2), ("rq", 1), ("side", 0),
    ("back", 0), ("r", 0), ("last", 0), ("own", 1), ("ro", 0), ("side", 1), ("back", 1), ("r", 1), ("n", 0),
    ("own", 2), ("side", 2), ("back", 2), ("r", 2), ("last", 1), ("n", 1), ("last", 2), ("n", 2),
)


def kernel(
    grid_rows, nh, hd,
    qkv, text, mask, out,
    q_s, kv_s, text_s, mask_s, mask_t, bias_s, m_s, l_s, acc_s, osend_s, orecv_s, lsend_s, lrecv_s, ofin_s, relay_q, relay_o,
    kv_sem, q_sem, text_sem, a2a_send,
    kv_send, kv_recv, q_send, q_recv, mk_send, mk_recv, o_send, o_recv, ls_send, ls_recv, out_send, out_sem, relay_sem,
):
    s, my = lax.axis_index("seq"), lax.axis_index("head")
    rows = qkv.shape[1]
    total = rows * nh
    tile = total // 2
    quarters = nh // CORES
    part = rows * CORES
    core, hi = my % CORES, my // CORES
    half = grid_rows * GW // 2
    lo, rest_s = s // half, s % half
    c = core * half + rest_s
    group = hi * 2 + lo
    row, col = c // GW, c % GW
    home = core == lo

    def holder(column):
        return (lo * half + column % half, hi * CORES + column // half)

    has = [[None, row > 0, row < grid_rows - 1], [None, col > 0, col < GW - 1]]
    dev = [[None, holder(c - GW), holder(c + GW)], [None, holder(c - 1), holder(c + 1)]]
    on_edge = [None, col == EDGE + 1, col == EDGE]

    def relays(i, heads):
        return [(RELAYS[0], EDGE + 1, 1, EDGE), (RELAYS[1], EDGE, 2, EDGE + 1)] if i in heads else []

    kv_axis = [MODES[i] for i in range(hd)]
    q_axis = [1 - MODES[i] for i in range(hd)]
    steps = [0] + sorted(range(1, quarters), key=lambda t: 2 * t == quarters)
    goes = []
    for t in steps:
        to = lax.rem(hi + quarters - t, quarters)
        for l in (lo, 1 - lo):
            goes.append((t, (l * half + rest_s, to * CORES + lo), to * 2 + l, t == 0 and l is lo))
    owners = [(core * half + rest_s, j) for j in range(nh)]
    my_rows = pl.ds(pl.multiple_of(my * rows, rows), rows)

    def lanes(h, i, n=1):
        return pl.ds(pl.multiple_of((h * hd + i) * HEAD_DIM, HEAD_DIM), n * HEAD_DIM)

    def at(i, n=1):
        return pl.ds(i * HEAD_DIM, n * HEAD_DIM)

    def remote(src, dst, ssem, rsem, device):
        pltpu.make_async_remote_copy(
            src_ref=src, dst_ref=dst, send_sem=ssem, recv_sem=rsem, device_id=device, device_id_type=MESH
        ).start()

    def wait(ref, sem):
        pltpu.make_async_copy(ref, ref, sem).wait()

    mate = (s, hi * CORES + 1 - core)
    across = ((1 - lo) * half + rest_s, my)

    barrier = pltpu.get_barrier_semaphore()
    count = len(goes) + quarters - home.astype(jnp.int32)
    for _, to, _, maybe in goes:
        if maybe:
            @pl.when(jnp.logical_not(home))
            def _():
                pl.semaphore_signal(barrier, inc=1, device_id=to, device_id_type=MESH)
        else:
            pl.semaphore_signal(barrier, inc=1, device_id=to, device_id_type=MESH)
    for t in range(quarters):
        pl.semaphore_signal(
            barrier, inc=1, device_id=(core * half + rest_s, t * CORES + 1 - lo), device_id_type=MESH
        )
    for a in (0, 1):
        for k in (1, 2):
            count = count + has[a][k].astype(jnp.int32)

            @pl.when(has[a][k])
            def _():
                pl.semaphore_signal(barrier, inc=1, device_id=dev[a][k], device_id_type=MESH)

    for at_col, to_col, slot, from_col in relays(0, (0,)):
        count = count + (col == from_col).astype(jnp.int32) + (col == at_col).astype(jnp.int32)

        @pl.when(col == at_col)
        def _():
            pl.semaphore_signal(barrier, inc=1, device_id=holder(c - at_col + from_col), device_id_type=MESH)

        @pl.when(col == to_col)
        def _():
            pl.semaphore_signal(barrier, inc=1, device_id=holder(c - to_col + at_col), device_id_type=MESH)

    @pl.when(home)
    def _():
        pltpu.make_async_copy(text, text_s, text_sem).start()

    mask_s[0] = jnp.zeros_like(mask_s[0])

    @pl.when(home)
    def _():
        mask_s[0, 0:2, 0:27] = mask[...]

    m_s[...] = jnp.full_like(m_s, NEG)
    l_s[...] = jnp.zeros_like(l_s)
    acc_s[...] = jnp.zeros_like(acc_s)
    for k in (1, 2):
        @pl.when(jnp.logical_not(has[1][k]))
        def _():
            q_s[k] = jnp.zeros_like(q_s[k])
            mask_s[2 + k] = jnp.zeros_like(mask_s[2 + k])

        @pl.when(jnp.logical_not(has[0][k]))
        def _():
            kv_s[k] = jnp.zeros_like(kv_s[k])

    pl.semaphore_wait(barrier, count)

    @pl.when(home)
    def _():
        mask_t[0] = mask_s[0]
        remote(mask_t.at[0], mask_t.at[1], mk_send.at[2, 0], mk_recv.at[2, 0], across)
        remote(text, text_s, mk_send.at[2, 1], text_sem, mate)

    def send(kind, i):
        for t, to, g, maybe in goes:
            if kind == 0:
                src, dst = qkv.at[0, :, lanes(g, i)], q_s.at[0, my_rows, at(i)]
                ssem, rsem = a2a_send.at[0, i], q_sem.at[i]
            else:
                src, dst = qkv.at[pl.ds(1, 2), :, lanes(g, i)], kv_s.at[0, :, my_rows, at(i)]
                ssem, rsem = a2a_send.at[1, i], kv_sem.at[i, t]
            if maybe:
                @pl.when(home)
                def _():
                    pltpu.make_async_copy(src, dst, rsem).start()

                @pl.when(jnp.logical_not(home))
                def _():
                    remote(src, dst, ssem, rsem, to)
            else:
                remote(src, dst, ssem, rsem, to)

    def sent(kind, i):
        sem = a2a_send.at[kind, i]
        block_of = (lambda n: q_s.at[0, pl.ds(0, n), at(i)]) if kind == 0 else (lambda n: kv_s.at[0, :, pl.ds(0, n), at(i)])

        @pl.when(home)
        def _():
            wait(block_of(total - rows), sem)

        @pl.when(jnp.logical_not(home))
        def _():
            wait(block_of(total), sem)

    def make_bias(mode, qs):
        which = 0 if qs == 0 else 1 + 2 * (1 - mode) + qs - 1
        lane = lax.broadcasted_iota(jnp.int32, (1, total), 1)
        for ks in range(3):
            for kf in range(2):
                picked = []
                for qf in range(2):
                    along_kv, along_q = (1, 0, 2)[ks], (1, 2, 0)[qs]
                    o = (kf - qf + 1) * 9 + (along_kv * 3 + along_q if mode == 0 else along_q * 3 + along_kv)
                    picked.append(jnp.broadcast_to(mask_s[which, qf:qf + 1, o:o + 1], (1, total)))
                chosen = jnp.where(lane < tile, picked[0], picked[1])
                bias_s[mode, qs, ks, kf] = jnp.where(chosen > 0, 0.0, NEG).astype(F32)

    def forward_kv(i, back):
        g = (hi + back) % quarters
        where = pl.ds(pl.multiple_of(g * part, part), part)
        wait(kv_s.at[0, :, where, at(i)], kv_sem.at[i, back])
        a = kv_axis[i]
        for k in (1, 2):
            @pl.when(has[a][k])
            def _():
                remote(
                    kv_s.at[0, :, where, at(i)], kv_s.at[3 - k, :, where, at(i)],
                    kv_send.at[i, k - 1], kv_recv.at[i, 2 - k], dev[a][k],
                )

    def forwarded_kv(i):
        for k in (1, 2):
            @pl.when(has[kv_axis[i]][k])
            def _():
                wait(kv_s.at[0, :, :, at(i)], kv_send.at[i, k - 1])

    def forward_q(i):
        wait(q_s.at[0, :, at(i)], q_sem.at[i])
        a = q_axis[i]
        for k in (1, 2):
            src, ssem = q_s.at[0, :, at(i)], q_send.at[i, k - 1]

            @pl.when(jnp.logical_and(has[a][k], jnp.logical_not(on_edge[k])) if i in RELAY_Q else has[a][k])
            def _():
                remote(src, q_s.at[3 - k, :, at(i)], ssem, q_recv.at[i, 2 - k], dev[a][k])

        for at_col, to_col, slot, from_col in relays(i, RELAY_Q):
            @pl.when(col == from_col)
            def _():
                remote(
                    q_s.at[0, :, at(i)], relay_q.at[i], q_send.at[i, 2 - slot], relay_sem.at[0, i], holder(c - from_col + at_col)
                )

    def pass_q(i):
        for at_col, to_col, slot, from_col in relays(i, RELAY_Q):
            @pl.when(col == at_col)
            def _():
                wait(relay_q.at[i], relay_sem.at[0, i])
                remote(
                    relay_q.at[i], q_s.at[slot, :, at(i)], relay_sem.at[1, i], q_recv.at[i, slot - 1],
                    holder(c - at_col + to_col),
                )

    def pass_o(i):
        for at_col, to_col, slot, from_col in relays(i, RELAY_O):
            @pl.when(col == at_col)
            def _():
                wait(relay_o.at[i], relay_sem.at[2, i])
                remote(
                    relay_o.at[i], orecv_s.at[slot - 1, i], relay_sem.at[3, i], o_recv.at[i, slot - 1],
                    holder(c - at_col + to_col),
                )

    def forwarded_q(i):
        for k in (1, 2):
            @pl.when(has[q_axis[i]][k])
            def _():
                wait(q_s.at[0, :, at(i)], q_send.at[i, k - 1])

    def update(i, jobs):
        scores, tops = [], []
        for qs, tiles in jobs:
            q = q_s[qs, :, at(i)]
            m_new = m_s[qs, i]
            mine = []
            for k, v, b in tiles:
                sc = lax.dot_general(k, q, (((1,), (1,)), ((), ())), preferred_element_type=F32)
                top = jnp.max(sc, axis=0, keepdims=True)
                m_new = jnp.maximum(m_new, top if b is None else top + b)
                mine.append(sc)
            scores.append(mine)
            tops.append(m_new)
        for (qs, tiles), mine, m_new in zip(jobs, scores, tops):
            alpha = jnp.exp2((m_s[qs, i] - m_new) * C2)
            big = m_new * C2
            l_new = l_s[qs, i] * alpha
            acc = acc_s[qs, i] * alpha
            for (k, v, b), sc in zip(tiles, mine):
                sub = big if b is None else jnp.where(b < 0, -NEG, big)
                e = jnp.exp2(sc * C2 - sub)
                l_new = l_new + jnp.sum(e, axis=0, keepdims=True)
                acc = acc + lax.dot_general(
                    v, e.astype(jnp.bfloat16), (((0,), (0,)), ((), ())), preferred_element_type=F32
                )
            m_s[qs, i] = m_new
            l_s[qs, i] = l_new
            acc_s[qs, i] = acc

    landed = set()

    def tiles_of(i, qs, ks):
        return [
            (kv_s[ks, 0, f * tile:(f + 1) * tile, at(i)], kv_s[ks, 1, f * tile:(f + 1) * tile, at(i)],
             bias_s[MODES[i], qs, ks, f])
            for f in range(2)
        ]

    def attend(i, slots, parts):
        for qs in slots:
            if qs and ("q", i, qs) not in landed:
                landed.add(("q", i, qs))

                @pl.when(has[q_axis[i]][qs])
                def _():
                    wait(q_s.at[qs, :, at(i)], q_recv.at[i, qs - 1])
        for ks in parts:
            if ks and ("kv", i, ks) not in landed:
                landed.add(("kv", i, ks))

                @pl.when(has[kv_axis[i]][ks])
                def _():
                    wait(kv_s.at[ks, :, :, at(i)], kv_recv.at[i, ks - 1])
        jobs = []
        for qs in slots:
            tiles = []
            for ks in parts:
                if ks is None:
                    tiles += [
                        (text_s[0, f * tile:(f + 1) * tile, at(i)], text_s[1, f * tile:(f + 1) * tile, at(i)], None)
                        for f in range(text_s.shape[1] // tile)
                    ]
                else:
                    tiles += tiles_of(i, qs, ks)
            jobs.append((qs, tiles))
        update(i, jobs)

    def remote_o(i, k):
        @pl.when(jnp.logical_not(on_edge[k]) if i in RELAY_O else has[1][k])
        def _():
            remote(
                osend_s.at[k - 1, i], orecv_s.at[2 - k, i], o_send.at[i, k - 1], o_recv.at[i, 2 - k], dev[1][k]
            )

    def give_back(i):
        a = q_axis[i]
        for k in (1, 2):
            @pl.when(has[a][k])
            def _():
                l = l_s[k, i]
                some = l > 0
                osend_s[k - 1, i] = (acc_s[k, i] * jnp.where(some, 1.0 / l, 0.0)).astype(jnp.bfloat16)
                lsend_s[k - 1, i] = jnp.broadcast_to(
                    jnp.where(some, m_s[k, i] * C2 + jnp.log2(l), NEG), lsend_s.shape[2:]
                )
                remote_o(i, k)
                remote(lsend_s.at[k - 1, i], lrecv_s.at[2 - k, i], ls_send.at[i, k - 1], ls_recv.at[i, 2 - k], dev[a][k])

        for at_col, to_col, slot, from_col in relays(i, RELAY_O):
            @pl.when(col == from_col)
            def _():
                remote(
                    osend_s.at[2 - slot, i], relay_o.at[i], o_send.at[i, 2 - slot], relay_sem.at[2, i],
                    holder(c - from_col + at_col),
                )

    def finish(i):
        a = q_axis[i]
        parts = []
        for k in (1, 2):
            @pl.when(has[a][k])
            def _():
                wait(orecv_s.at[k - 1, i], o_recv.at[i, k - 1])
                wait(lrecv_s.at[k - 1, i], ls_recv.at[i, k - 1])

            @pl.when(jnp.logical_not(has[a][k]))
            def _():
                orecv_s[k - 1, i] = jnp.zeros_like(orecv_s[k - 1, i])
                lrecv_s[k - 1, i] = jnp.full_like(lrecv_s[k - 1, i], NEG)

            parts.append((lrecv_s[k - 1, i, 0:1], orecv_s[k - 1, i].astype(F32)))
        l = l_s[0, i]
        lse = m_s[0, i] * C2 + jnp.log2(l)
        top = jnp.maximum(lse, jnp.maximum(parts[0][0], parts[1][0]))
        w = jnp.exp2(lse - top)
        w1, w2 = jnp.exp2(parts[0][0] - top), jnp.exp2(parts[1][0] - top)
        scale = 1.0 / (w + w1 + w2)
        o = acc_s[0, i] * (w * scale / l) + parts[0][1] * (w1 * scale) + parts[1][1] * (w2 * scale)
        ofin_s[:, at(i)] = o.T.astype(jnp.bfloat16)
        for j, to in enumerate(owners):
            src, dst = ofin_s.at[pl.ds(j * rows, rows), at(i)], out.at[:, lanes(group, i)]
            mine = jnp.logical_and(home, my == j)

            @pl.when(mine)
            def _():
                pltpu.make_async_copy(src, dst, out_sem).start()

            @pl.when(jnp.logical_not(mine))
            def _():
                remote(src, dst, out_send, out_sem, to)

    def masks():
        @pl.when(jnp.logical_not(home))
        def _():
            wait(mask_t.at[1], mk_recv.at[2, 0])
            mask_s[0] = mask_t[1]

        for a in (0, 1):
            for k in (1, 2):
                @pl.when(has[a][k])
                def _():
                    remote(
                        mask_s.at[0], mask_s.at[1 + 2 * a + 2 - k], mk_send.at[a, k - 1], mk_recv.at[a, 2 - k], dev[a][k]
                    )

    def biases():
        for mode in sorted(set(MODES)):
            make_bias(mode, 0)
            for k in (1, 2):
                @pl.when(has[1 - mode][k])
                def _():
                    wait(mask_s.at[1 + 2 * (1 - mode) + k - 1], mk_recv.at[1 - mode, k - 1])

                make_bias(mode, k)

    first = True
    kinds = {"q": 0, "kv": 1}
    for op, *rest in PLAN:
        if op == "y":
            send(kinds[rest[0]], rest[1])
        elif op == "ys":
            sent(kinds[rest[0]], rest[1])
        elif op == "f":
            if first:
                first = False
                forward_kv(*rest)
                masks()
                biases()
                wait(text_s, text_sem)
            else:
                forward_kv(*rest)
        elif op == "fs":
            forwarded_kv(rest[0])
        elif op == "q":
            forward_q(rest[0])
        elif op == "qs":
            forwarded_q(rest[0])
        elif op == "own":
            attend(rest[0], (0,), (None, 0))
        elif op == "side":
            attend(rest[0], (1, 2), (0,))
        elif op == "back":
            attend(rest[0], (1, 2), (1, 2))
        elif op == "last":
            attend(rest[0], (0,), (1, 2))
        elif op == "r":
            give_back(rest[0])
        elif op == "rq":
            pass_q(rest[0])
        elif op == "ro":
            pass_o(rest[0])
        elif op == "n":
            finish(rest[0])

    @pl.when(home)
    def _():
        wait(mask_t.at[0], mk_send.at[2, 0])
        wait(text_s, mk_send.at[2, 1])
        wait(ofin_s.at[pl.ds(0, total - rows), :], out_send)

    @pl.when(jnp.logical_not(home))
    def _():
        wait(ofin_s, out_send)

    for i in RELAY_Q:
        for at_col, to_col, slot, from_col in relays(i, RELAY_Q):
            @pl.when(col == at_col)
            def _():
                wait(relay_q.at[i], relay_sem.at[1, i])

    for i in RELAY_O:
        for at_col, to_col, slot, from_col in relays(i, RELAY_O):
            @pl.when(col == at_col)
            def _():
                wait(relay_o.at[i], relay_sem.at[3, i])

    for i in range(hd):
        for kind, name in ((0, "q"), (1, "kv")):
            if ("ys", name, i) not in PLAN:
                sent(kind, i)
        if ("fs", i) not in PLAN:
            forwarded_kv(i)
        if ("qs", i) not in PLAN:
            forwarded_q(i)
        for k in (1, 2):
            @pl.when(has[q_axis[i]][k])
            def _():
                wait(osend_s.at[k - 1, i], o_send.at[i, k - 1])
                wait(lsend_s.at[k - 1, i], ls_send.at[i, k - 1])
    for a in (0, 1):
        for k in (1, 2):
            @pl.when(has[a][k])
            def _():
                wait(mask_s.at[0], mk_send.at[a, k - 1])
                if 1 - a not in MODES:
                    wait(mask_s.at[1 + 2 * a + k - 1], mk_recv.at[a, k - 1])
    wait(out, out_sem)


def solution(mesh):
    nh = mesh.shape["head"]
    grid_rows = mesh.shape["seq"] // GW

    def on_device(qkv, text_kv, window_mask):
        _, rows, d = qkv.shape
        txt, width = text_kv.shape[1:]
        hd = width // HEAD_DIM
        total = rows * nh
        quarters = nh // CORES
        bf = jnp.bfloat16
        dma = pltpu.SemaphoreType.DMA
        return pl.pallas_call(
            functools.partial(kernel, grid_rows, nh, hd),
            out_shape=jax.ShapeDtypeStruct((rows, d), bf),
            in_specs=[
                pl.BlockSpec(memory_space=pl.ANY),
                pl.BlockSpec(memory_space=pl.ANY),
                pl.BlockSpec(memory_space=pltpu.VMEM),
            ],
            out_specs=pl.BlockSpec(memory_space=pltpu.VMEM),
            scratch_shapes=[
                pltpu.VMEM((3, total, width), bf),
                pltpu.VMEM((3, 2, total, width), bf),
                pltpu.VMEM((2, txt, width), bf),
                pltpu.VMEM((5, 8, 128), jnp.int32),
                pltpu.VMEM((2, 8, 128), jnp.int32),
                pltpu.VMEM((2, 3, 3, 2, 1, total), F32),
                pltpu.VMEM((3, hd, 1, total), F32),
                pltpu.VMEM((3, hd, 1, total), F32),
                pltpu.VMEM((3, hd, HEAD_DIM, total), F32),
                pltpu.VMEM((2, hd, HEAD_DIM, total), bf),
                pltpu.VMEM((2, hd, HEAD_DIM, total), bf),
                pltpu.VMEM((2, hd, 8, total), F32),
                pltpu.VMEM((2, hd, 8, total), F32),
                pltpu.VMEM((total, width), bf),
                pltpu.VMEM((hd, total, HEAD_DIM), bf),
                pltpu.VMEM((hd, HEAD_DIM, total), bf),
                dma((hd, quarters)), dma((hd,)), dma, dma((2, hd)),
                dma((hd, 2)), dma((hd, 2)), dma((hd, 2)), dma((hd, 2)), dma((3, 2)), dma((3, 2)),
                dma((hd, 2)), dma((hd, 2)), dma((hd, 2)), dma((hd, 2)), dma, dma, dma((4, hd)),
            ],
            compiler_params=pltpu.CompilerParams(
                collective_id=0, has_side_effects=True, vmem_limit_bytes=60 << 20
            ),
            cost_estimate=pl.CostEstimate(
                flops=4 * total * hd * HEAD_DIM * (9 * total + txt),
                bytes_accessed=8 * rows * d,
                transcendentals=total * hd * (9 * total + txt),
            ),
        )(qkv, text_kv, window_mask)

    return jax.shard_map(
        on_device, mesh=mesh,
        in_specs=(P(None, ("seq", "head"), None), P(None, None, "head"), P("seq", None)),
        out_specs=P(("seq", "head"), None), check_vma=False,
    )
```

```python
import functools
import math

import jax
import jax.numpy as jnp
from jax import lax
from jax.experimental import pallas as pl
from jax.experimental.pallas import tpu as pltpu
from jax.sharding import PartitionSpec as P

HEAD_DIM = 128
GW = 8
CORES = 2
MESH = pl.DeviceIdType.MESH
NEG = -1e30
C2 = math.log2(math.e) / math.sqrt(HEAD_DIM)
F32 = jnp.float32
MODES = (0, 0, 0)
EDGE = GW // 2 - 1
RELAYS = (0, 7)
RELAY_Q = (0, 1)
RELAY_O = (0,)
PLAN = (
    ("y", "kv", 0), ("f", 0, 0), ("y", "q", 0), ("y", "kv", 1), ("y", "q", 1), ("y", "kv", 2), ("y", "q", 2),
    ("f", 0, 1), ("f", 0, 3), ("f", 0, 2), ("q", 0), ("f", 1, 0), ("f", 1, 1), ("f", 1, 3), ("f", 1, 2), ("rq", 0),
    ("q", 1), ("f", 2, 0), ("own", 0), ("f", 2, 1), ("f", 2, 3), ("f", 2, 2), ("q", 2), ("rq", 1), ("side", 0),
    ("back", 0), ("r", 0), ("last", 0), ("own", 1), ("ro", 0), ("side", 1), ("back", 1), ("r", 1), ("n", 0),
    ("own", 2), ("side", 2), ("back", 2), ("r", 2), ("last", 1), ("n", 1), ("last", 2), ("n", 2),
)


def kernel(
    grid_rows, nh, hd,
    qkv, text, mask, out,
    q_s, kv_s, text_s, mask_s, mask_t, bias_s, m_s, l_s, acc_s, osend_s, orecv_s, lsend_s, lrecv_s, ofin_s, relay_q, relay_o,
    kv_sem, q_sem, text_sem, a2a_send,
    kv_send, kv_recv, q_send, q_recv, mk_send, mk_recv, o_send, o_recv, ls_send, ls_recv, out_send, out_sem, relay_sem,
):
    s, my = lax.axis_index("seq"), lax.axis_index("head")
    rows = qkv.shape[1]
    total = rows * nh
    tile = total // 2
    quarters = nh // CORES
    part = rows * CORES
    core, hi = my % CORES, my // CORES
    half = grid_rows * GW // 2
    lo, rest_s = s // half, s % half
    c = core * half + rest_s
    group = hi * 2 + lo
    row, col = c // GW, c % GW
    home = core == lo

    def holder(column):
        return (lo * half + column % half, hi * CORES + column // half)

    has = [[None, row > 0, row < grid_rows - 1], [None, col > 0, col < GW - 1]]
    dev = [[None, holder(c - GW), holder(c + GW)], [None, holder(c - 1), holder(c + 1)]]
    on_edge = [None, col == EDGE + 1, col == EDGE]

    def relays(i, heads):
        return [(RELAYS[0], EDGE + 1, 1, EDGE), (RELAYS[1], EDGE, 2, EDGE + 1)] if i in heads else []

    kv_axis = [MODES[i] for i in range(hd)]
    q_axis = [1 - MODES[i] for i in range(hd)]
    steps = [0] + sorted(range(1, quarters), key=lambda t: 2 * t == quarters)
    goes = []
    for t in steps:
        to = lax.rem(hi + quarters - t, quarters)
        for l in (lo, 1 - lo):
            goes.append((t, (l * half + rest_s, to * CORES + lo), to * 2 + l, t == 0 and l is lo))
    owners = [(core * half + rest_s, j) for j in range(nh)]
    my_rows = pl.ds(pl.multiple_of(my * rows, rows), rows)

    def lanes(h, i, n=1):
        return pl.ds(pl.multiple_of((h * hd + i) * HEAD_DIM, HEAD_DIM), n * HEAD_DIM)

    def at(i, n=1):
        return pl.ds(i * HEAD_DIM, n * HEAD_DIM)

    def remote(src, dst, ssem, rsem, device):
        pltpu.make_async_remote_copy(
            src_ref=src, dst_ref=dst, send_sem=ssem, recv_sem=rsem, device_id=device, device_id_type=MESH
        ).start()

    def wait(ref, sem):
        pltpu.make_async_copy(ref, ref, sem).wait()

    mate = (s, hi * CORES + 1 - core)
    across = ((1 - lo) * half + rest_s, my)

    barrier = pltpu.get_barrier_semaphore()
    count = len(goes) + quarters - home.astype(jnp.int32)
    for _, to, _, maybe in goes:
        if maybe:
            @pl.when(jnp.logical_not(home))
            def _():
                pl.semaphore_signal(barrier, inc=1, device_id=to, device_id_type=MESH)
        else:
            pl.semaphore_signal(barrier, inc=1, device_id=to, device_id_type=MESH)
    for t in range(quarters):
        pl.semaphore_signal(
            barrier, inc=1, device_id=(core * half + rest_s, t * CORES + 1 - lo), device_id_type=MESH
        )
    for a in (0, 1):
        for k in (1, 2):
            count = count + has[a][k].astype(jnp.int32)

            @pl.when(has[a][k])
            def _():
                pl.semaphore_signal(barrier, inc=1, device_id=dev[a][k], device_id_type=MESH)

    for at_col, to_col, slot, from_col in relays(0, (0,)):
        count = count + (col == from_col).astype(jnp.int32) + (col == at_col).astype(jnp.int32)

        @pl.when(col == at_col)
        def _():
            pl.semaphore_signal(barrier, inc=1, device_id=holder(c - at_col + from_col), device_id_type=MESH)

        @pl.when(col == to_col)
        def _():
            pl.semaphore_signal(barrier, inc=1, device_id=holder(c - to_col + at_col), device_id_type=MESH)

    @pl.when(home)
    def _():
        pltpu.make_async_copy(text, text_s, text_sem).start()

    mask_s[0] = jnp.zeros_like(mask_s[0])

    @pl.when(home)
    def _():
        mask_s[0, 0:2, 0:27] = mask[...]

    m_s[...] = jnp.full_like(m_s, NEG)
    l_s[...] = jnp.zeros_like(l_s)
    acc_s[...] = jnp.zeros_like(acc_s)
    for k in (1, 2):
        @pl.when(jnp.logical_not(has[1][k]))
        def _():
            q_s[k] = jnp.zeros_like(q_s[k])
            mask_s[2 + k] = jnp.zeros_like(mask_s[2 + k])

        @pl.when(jnp.logical_not(has[0][k]))
        def _():
            kv_s[k] = jnp.zeros_like(kv_s[k])

    pl.semaphore_wait(barrier, count)

    @pl.when(home)
    def _():
        mask_t[0] = mask_s[0]
        remote(mask_t.at[0], mask_t.at[1], mk_send.at[2, 0], mk_recv.at[2, 0], across)
        remote(text, text_s, mk_send.at[2, 1], text_sem, mate)

    def send(kind, i):
        for t, to, g, maybe in goes:
            if kind == 0:
                src, dst = qkv.at[0, :, lanes(g, i)], q_s.at[0, my_rows, at(i)]
                ssem, rsem = a2a_send.at[0, i], q_sem.at[i]
            else:
                src, dst = qkv.at[pl.ds(1, 2), :, lanes(g, i)], kv_s.at[0, :, my_rows, at(i)]
                ssem, rsem = a2a_send.at[1, i], kv_sem.at[i, t]
            if maybe:
                @pl.when(home)
                def _():
                    pltpu.make_async_copy(src, dst, rsem).start()

                @pl.when(jnp.logical_not(home))
                def _():
                    remote(src, dst, ssem, rsem, to)
            else:
                remote(src, dst, ssem, rsem, to)

    def sent(kind, i):
        sem = a2a_send.at[kind, i]
        block_of = (lambda n: q_s.at[0, pl.ds(0, n), at(i)]) if kind == 0 else (lambda n: kv_s.at[0, :, pl.ds(0, n), at(i)])

        @pl.when(home)
        def _():
            wait(block_of(total - rows), sem)

        @pl.when(jnp.logical_not(home))
        def _():
            wait(block_of(total), sem)

    def make_bias(mode, qs):
        which = 0 if qs == 0 else 1 + 2 * (1 - mode) + qs - 1
        lane = lax.broadcasted_iota(jnp.int32, (1, total), 1)
        for ks in range(3):
            for kf in range(2):
                picked = []
                for qf in range(2):
                    along_kv, along_q = (1, 0, 2)[ks], (1, 2, 0)[qs]
                    o = (kf - qf + 1) * 9 + (along_kv * 3 + along_q if mode == 0 else along_q * 3 + along_kv)
                    picked.append(jnp.broadcast_to(mask_s[which, qf:qf + 1, o:o + 1], (1, total)))
                chosen = jnp.where(lane < tile, picked[0], picked[1])
                bias_s[mode, qs, ks, kf] = jnp.where(chosen > 0, 0.0, NEG).astype(F32)

    def forward_kv(i, back):
        g = (hi + back) % quarters
        where = pl.ds(pl.multiple_of(g * part, part), part)
        wait(kv_s.at[0, :, where, at(i)], kv_sem.at[i, back])
        a = kv_axis[i]
        for k in (1, 2):
            @pl.when(has[a][k])
            def _():
                remote(
                    kv_s.at[0, :, where, at(i)], kv_s.at[3 - k, :, where, at(i)],
                    kv_send.at[i, k - 1], kv_recv.at[i, 2 - k], dev[a][k],
                )

    def forwarded_kv(i):
        for k in (1, 2):
            @pl.when(has[kv_axis[i]][k])
            def _():
                wait(kv_s.at[0, :, :, at(i)], kv_send.at[i, k - 1])

    def forward_q(i):
        wait(q_s.at[0, :, at(i)], q_sem.at[i])
        a = q_axis[i]
        for k in (1, 2):
            src, ssem = q_s.at[0, :, at(i)], q_send.at[i, k - 1]

            @pl.when(jnp.logical_and(has[a][k], jnp.logical_not(on_edge[k])) if i in RELAY_Q else has[a][k])
            def _():
                remote(src, q_s.at[3 - k, :, at(i)], ssem, q_recv.at[i, 2 - k], dev[a][k])

        for at_col, to_col, slot, from_col in relays(i, RELAY_Q):
            @pl.when(col == from_col)
            def _():
                remote(
                    q_s.at[0, :, at(i)], relay_q.at[i], q_send.at[i, 2 - slot], relay_sem.at[0, i], holder(c - from_col + at_col)
                )

    def pass_q(i):
        for at_col, to_col, slot, from_col in relays(i, RELAY_Q):
            @pl.when(col == at_col)
            def _():
                wait(relay_q.at[i], relay_sem.at[0, i])
                remote(
                    relay_q.at[i], q_s.at[slot, :, at(i)], relay_sem.at[1, i], q_recv.at[i, slot - 1],
                    holder(c - at_col + to_col),
                )

    def pass_o(i):
        for at_col, to_col, slot, from_col in relays(i, RELAY_O):
            @pl.when(col == at_col)
            def _():
                wait(relay_o.at[i], relay_sem.at[2, i])
                remote(
                    relay_o.at[i], orecv_s.at[slot - 1, i], relay_sem.at[3, i], o_recv.at[i, slot - 1],
                    holder(c - at_col + to_col),
                )

    def forwarded_q(i):
        for k in (1, 2):
            @pl.when(has[q_axis[i]][k])
            def _():
                wait(q_s.at[0, :, at(i)], q_send.at[i, k - 1])

    def update(i, jobs):
        scores, tops = [], []
        for qs, tiles in jobs:
            q = q_s[qs, :, at(i)]
            m_new = m_s[qs, i]
            mine = []
            for k, v, b in tiles:
                sc = lax.dot_general(k, q, (((1,), (1,)), ((), ())), preferred_element_type=F32)
                top = jnp.max(sc, axis=0, keepdims=True)
                m_new = jnp.maximum(m_new, top if b is None else top + b)
                mine.append(sc)
            scores.append(mine)
            tops.append(m_new)
        for (qs, tiles), mine, m_new in zip(jobs, scores, tops):
            alpha = jnp.exp2((m_s[qs, i] - m_new) * C2)
            big = m_new * C2
            l_new = l_s[qs, i] * alpha
            acc = acc_s[qs, i] * alpha
            for (k, v, b), sc in zip(tiles, mine):
                sub = big if b is None else jnp.where(b < 0, -NEG, big)
                e = jnp.exp2(sc * C2 - sub)
                l_new = l_new + jnp.sum(e, axis=0, keepdims=True)
                acc = acc + lax.dot_general(
                    v, e.astype(jnp.bfloat16), (((0,), (0,)), ((), ())), preferred_element_type=F32
                )
            m_s[qs, i] = m_new
            l_s[qs, i] = l_new
            acc_s[qs, i] = acc

    landed = set()

    def tiles_of(i, qs, ks):
        return [
            (kv_s[ks, 0, f * tile:(f + 1) * tile, at(i)], kv_s[ks, 1, f * tile:(f + 1) * tile, at(i)],
             bias_s[MODES[i], qs, ks, f])
            for f in range(2)
        ]

    def attend(i, slots, parts):
        for qs in slots:
            if qs and ("q", i, qs) not in landed:
                landed.add(("q", i, qs))

                @pl.when(has[q_axis[i]][qs])
                def _():
                    wait(q_s.at[qs, :, at(i)], q_recv.at[i, qs - 1])
        for ks in parts:
            if ks and ("kv", i, ks) not in landed:
                landed.add(("kv", i, ks))

                @pl.when(has[kv_axis[i]][ks])
                def _():
                    wait(kv_s.at[ks, :, :, at(i)], kv_recv.at[i, ks - 1])
        jobs = []
        for qs in slots:
            tiles = []
            for ks in parts:
                if ks is None:
                    tiles += [
                        (text_s[0, f * tile:(f + 1) * tile, at(i)], text_s[1, f * tile:(f + 1) * tile, at(i)], None)
                        for f in range(text_s.shape[1] // tile)
                    ]
                else:
                    tiles += tiles_of(i, qs, ks)
            jobs.append((qs, tiles))
        update(i, jobs)

    def remote_o(i, k):
        @pl.when(jnp.logical_not(on_edge[k]) if i in RELAY_O else has[1][k])
        def _():
            remote(
                osend_s.at[k - 1, i], orecv_s.at[2 - k, i], o_send.at[i, k - 1], o_recv.at[i, 2 - k], dev[1][k]
            )

    def give_back(i):
        a = q_axis[i]
        for k in (1, 2):
            @pl.when(has[a][k])
            def _():
                l = l_s[k, i]
                some = l > 0
                osend_s[k - 1, i] = (acc_s[k, i] * jnp.where(some, 1.0 / l, 0.0)).astype(jnp.bfloat16)
                lsend_s[k - 1, i] = jnp.broadcast_to(
                    jnp.where(some, m_s[k, i] * C2 + jnp.log2(l), NEG), lsend_s.shape[2:]
                )
                remote_o(i, k)
                remote(lsend_s.at[k - 1, i], lrecv_s.at[2 - k, i], ls_send.at[i, k - 1], ls_recv.at[i, 2 - k], dev[a][k])

        for at_col, to_col, slot, from_col in relays(i, RELAY_O):
            @pl.when(col == from_col)
            def _():
                remote(
                    osend_s.at[2 - slot, i], relay_o.at[i], o_send.at[i, 2 - slot], relay_sem.at[2, i],
                    holder(c - from_col + at_col),
                )

    def finish(i):
        a = q_axis[i]
        parts = []
        for k in (1, 2):
            @pl.when(has[a][k])
            def _():
                wait(orecv_s.at[k - 1, i], o_recv.at[i, k - 1])
                wait(lrecv_s.at[k - 1, i], ls_recv.at[i, k - 1])

            @pl.when(jnp.logical_not(has[a][k]))
            def _():
                orecv_s[k - 1, i] = jnp.zeros_like(orecv_s[k - 1, i])
                lrecv_s[k - 1, i] = jnp.full_like(lrecv_s[k - 1, i], NEG)

            parts.append((lrecv_s[k - 1, i, 0:1], orecv_s[k - 1, i].astype(F32)))
        l = l_s[0, i]
        lse = m_s[0, i] * C2 + jnp.log2(l)
        top = jnp.maximum(lse, jnp.maximum(parts[0][0], parts[1][0]))
        w = jnp.exp2(lse - top)
        w1, w2 = jnp.exp2(parts[0][0] - top), jnp.exp2(parts[1][0] - top)
        scale = 1.0 / (w + w1 + w2)
        o = acc_s[0, i] * (w * scale / l) + parts[0][1] * (w1 * scale) + parts[1][1] * (w2 * scale)
        ofin_s[:, at(i)] = o.T.astype(jnp.bfloat16)
        for j, to in enumerate(owners):
            src, dst = ofin_s.at[pl.ds(j * rows, rows), at(i)], out.at[:, lanes(group, i)]
            mine = jnp.logical_and(home, my == j)

            @pl.when(mine)
            def _():
                pltpu.make_async_copy(src, dst, out_sem).start()

            @pl.when(jnp.logical_not(mine))
            def _():
                remote(src, dst, out_send, out_sem, to)

    def masks():
        @pl.when(jnp.logical_not(home))
        def _():
            wait(mask_t.at[1], mk_recv.at[2, 0])
            mask_s[0] = mask_t[1]

        for a in (0, 1):
            for k in (1, 2):
                @pl.when(has[a][k])
                def _():
                    remote(
                        mask_s.at[0], mask_s.at[1 + 2 * a + 2 - k], mk_send.at[a, k - 1], mk_recv.at[a, 2 - k], dev[a][k]
                    )

    def biases():
        for mode in sorted(set(MODES)):
            make_bias(mode, 0)
            for k in (1, 2):
                @pl.when(has[1 - mode][k])
                def _():
                    wait(mask_s.at[1 + 2 * (1 - mode) + k - 1], mk_recv.at[1 - mode, k - 1])

                make_bias(mode, k)

    first = True
    kinds = {"q": 0, "kv": 1}
    for op, *rest in PLAN:
        if op == "y":
            send(kinds[rest[0]], rest[1])
        elif op == "ys":
            sent(kinds[rest[0]], rest[1])
        elif op == "f":
            if first:
                first = False
                forward_kv(*rest)
                masks()
                biases()
                wait(text_s, text_sem)
            else:
                forward_kv(*rest)
        elif op == "fs":
            forwarded_kv(rest[0])
        elif op == "q":
            forward_q(rest[0])
        elif op == "qs":
            forwarded_q(rest[0])
        elif op == "own":
            attend(rest[0], (0,), (None, 0))
        elif op == "side":
            attend(rest[0], (1, 2), (0,))
        elif op == "back":
            attend(rest[0], (1, 2), (1, 2))
        elif op == "last":
            attend(rest[0], (0,), (1, 2))
        elif op == "r":
            give_back(rest[0])
        elif op == "rq":
            pass_q(rest[0])
        elif op == "ro":
            pass_o(rest[0])
        elif op == "n":
            finish(rest[0])

    @pl.when(home)
    def _():
        wait(mask_t.at[0], mk_send.at[2, 0])
        wait(text_s, mk_send.at[2, 1])
        wait(ofin_s.at[pl.ds(0, total - rows), :], out_send)

    @pl.when(jnp.logical_not(home))
    def _():
        wait(ofin_s, out_send)

    for i in RELAY_Q:
        for at_col, to_col, slot, from_col in relays(i, RELAY_Q):
            @pl.when(col == at_col)
            def _():
                wait(relay_q.at[i], relay_sem.at[1, i])

    for i in RELAY_O:
        for at_col, to_col, slot, from_col in relays(i, RELAY_O):
            @pl.when(col == at_col)
            def _():
                wait(relay_o.at[i], relay_sem.at[3, i])

    for i in range(hd):
        for kind, name in ((0, "q"), (1, "kv")):
            if ("ys", name, i) not in PLAN:
                sent(kind, i)
        if ("fs", i) not in PLAN:
            forwarded_kv(i)
        if ("qs", i) not in PLAN:
            forwarded_q(i)
        for k in (1, 2):
            @pl.when(has[q_axis[i]][k])
            def _():
                wait(osend_s.at[k - 1, i], o_send.at[i, k - 1])
                wait(lsend_s.at[k - 1, i], ls_send.at[i, k - 1])
    for a in (0, 1):
        for k in (1, 2):
            @pl.when(has[a][k])
            def _():
                wait(mask_s.at[0], mk_send.at[a, k - 1])
                if 1 - a not in MODES:
                    wait(mask_s.at[1 + 2 * a + k - 1], mk_recv.at[a, k - 1])
    wait(out, out_sem)


def solution(mesh):
    nh = mesh.shape["head"]
    grid_rows = mesh.shape["seq"] // GW

    def on_device(qkv, text_kv, window_mask):
        _, rows, d = qkv.shape
        txt, width = text_kv.shape[1:]
        hd = width // HEAD_DIM
        total = rows * nh
        quarters = nh // CORES
        bf = jnp.bfloat16
        dma = pltpu.SemaphoreType.DMA
        return pl.pallas_call(
            functools.partial(kernel, grid_rows, nh, hd),
            out_shape=jax.ShapeDtypeStruct((rows, d), bf),
            in_specs=[
                pl.BlockSpec(memory_space=pl.ANY),
                pl.BlockSpec(memory_space=pl.ANY),
                pl.BlockSpec(memory_space=pltpu.VMEM),
            ],
            out_specs=pl.BlockSpec(memory_space=pl.ANY),
            scratch_shapes=[
                pltpu.VMEM((3, total, width), bf),
                pltpu.VMEM((3, 2, total, width), bf),
                pltpu.VMEM((2, txt, width), bf),
                pltpu.VMEM((5, 8, 128), jnp.int32),
                pltpu.VMEM((2, 8, 128), jnp.int32),
                pltpu.VMEM((2, 3, 3, 2, 1, total), F32),
                pltpu.VMEM((3, hd, 1, total), F32),
                pltpu.VMEM((3, hd, 1, total), F32),
                pltpu.VMEM((3, hd, HEAD_DIM, total), F32),
                pltpu.VMEM((2, hd, HEAD_DIM, total), bf),
                pltpu.VMEM((2, hd, HEAD_DIM, total), bf),
                pltpu.VMEM((2, hd, 8, total), F32),
                pltpu.VMEM((2, hd, 8, total), F32),
                pltpu.VMEM((total, width), bf),
                pltpu.VMEM((hd, total, HEAD_DIM), bf),
                pltpu.VMEM((hd, HEAD_DIM, total), bf),
                dma((hd, quarters)), dma((hd,)), dma, dma((2, hd)),
                dma((hd, 2)), dma((hd, 2)), dma((hd, 2)), dma((hd, 2)), dma((3, 2)), dma((3, 2)),
                dma((hd, 2)), dma((hd, 2)), dma((hd, 2)), dma((hd, 2)), dma, dma, dma((4, hd)),
            ],
            compiler_params=pltpu.CompilerParams(
                collective_id=0, has_side_effects=True, vmem_limit_bytes=60 << 20
            ),
            cost_estimate=pl.CostEstimate(
                flops=4 * total * hd * HEAD_DIM * (9 * total + txt),
                bytes_accessed=8 * rows * d,
                transcendentals=total * hd * (9 * total + txt),
            ),
        )(qkv, text_kv, window_mask)

    return jax.shard_map(
        on_device, mesh=mesh,
        in_specs=(P(None, ("seq", "head"), None), P(None, None, "head"), P("seq", None)),
        out_specs=P(("seq", "head"), None), check_vma=False,
    )
```
